128 devices in a mesh: section: 64 (over z, y, x), tp: 2 (over core).
Axes of the slice: x: 4, y: 4, z: 4, core: 2. Of those that a mesh axis runs over, the one named last changes fastest.
Arguments:
- partials: bfloat16 [64, 2, 512, 8192], P('section', 'tp'), may hold values from -30 to 30
- kept_positions: int32 [64, 512], replicated, may hold values from 0 to 4095, as said below
- destination: int32 [64, 512], replicated, may hold values from 0 to 63, as said below
- slot_index: int32 [64, 512], replicated, may hold values from 0 to 511, as said below
- query_scale: float32 [8192], P('tp'), may hold values from -1.5 to 1.5
- key_scale: float32 [8192], P('tp'), may hold values from -1.5 to 1.5
Outputs:
- attended: bfloat16 [32768, 8192], P('section', 'tp')
The draws below stay inside these ranges and needn't reach their ends.
Inputs may be any that keep to these rules, and one draw needn't show every extreme that they name: `destination`: each source segment sends exactly 8 of its rows to every segment, itself included; every segment receives exactly 512 rows. `slot_index`: the rows arriving at one segment have distinct slots. `kept_positions`: distinct within a segment's microbatch.
All inputs are finite; a program needn't handle non-finite values.
Results may differ from the reference program's by a relative error of at most 0.0075.
Values may be sent and summed in bfloat16 or wider, within the bound.
A program may use at most 192 MiB of HBM per device.

```python
import math
import jax
import jax.numpy as jnp
from jax import lax

HD = 128
CAP = 8
D = 8192
KEPT = 512
SEQ = 4096
N_SECTION = 64
N_TP = 2


def routing(key):
    second, third = jax.random.split(key, 2)
    inverse = jax.vmap(lambda k: jax.random.permutation(k, KEPT))(jax.random.split(second, N_SECTION))
    target = inverse // CAP
    within = jnp.arange(N_SECTION)[:, None] * CAP + inverse % CAP
    shuffle = jax.vmap(lambda k: jax.random.permutation(k, KEPT))(jax.random.split(third, N_SECTION))
    placed = shuffle[target, within]
    return (target.astype(jnp.int32), placed.astype(jnp.int32))


def draw_destination(key, part):
    return routing(key)[0]


def draw_slot_index(key, part):
    return routing(key)[1]


def draw_kept_positions(key, part):
    key = jax.random.fold_in(key, 2)
    chosen = jax.vmap(lambda k: jax.random.permutation(k, SEQ)[:KEPT])(jax.random.split(key, N_SECTION))
    return chosen.astype(jnp.int32)


def draw_partials(key, part):
    key = jax.random.fold_in(key, 4)
    keys = jax.random.split(key, 1)
    column = jnp.arange(D, dtype=jnp.float32) / D
    base = jax.random.normal(keys[0], (N_SECTION, N_TP, KEPT, D), jnp.float32)
    values = base * 0.35 * jnp.sqrt(1.0 + 2.0 * column)
    return jnp.clip(values, -28.0, 28.0).astype(jnp.bfloat16)


def block_levels(rng, dims, pieces, least, top_value):
    gain = 1.0
    for dim, shards_of in pieces:
        draws = jax.random.uniform(jax.random.fold_in(jax.random.fold_in(rng, 6), dim), (shards_of,), jnp.float32, least / len(pieces), top_value / len(pieces))
        gain = gain * jnp.repeat(jnp.exp(draws), dims[dim] // shards_of).reshape((-1,) + (1,) * (len(dims) - 1 - dim))
    return gain


def setup_inputs(seed: int = 0) -> dict:
    seeds = jax.random.split(jax.random.key(seed), 7)
    partials = draw_partials(jax.random.fold_in(seeds[6], 71), 0)
    kept_positions = draw_kept_positions(jax.random.fold_in(seeds[6], 71), 0)
    destination = draw_destination(jax.random.fold_in(seeds[6], 71), 0)
    slot_index = draw_slot_index(jax.random.fold_in(seeds[6], 71), 0)
    query_scale = jnp.clip(jax.random.uniform(seeds[4], (D,), jnp.float32, -1.5, 1.5) * block_levels(seeds[4], (D,), ((0, 2),), -0.4, 0.0), -1.5, 1.5)
    key_scale = jnp.clip(jax.random.uniform(seeds[5], (D,), jnp.float32, -1.5, 1.5) * block_levels(seeds[5], (D,), ((0, 2),), -0.4, 0.0), -1.5, 1.5)
    return dict(partials=partials, kept_positions=kept_positions, destination=destination, slot_index=slot_index, query_scale=query_scale, key_scale=key_scale)


eps = 1e-05
theta = 500000.0

def rotate(values, positions):
    half = values.shape[-1] // 2
    freq = jnp.exp(jnp.arange(half, dtype=jnp.float32) * (-2.0 * math.log(theta) / values.shape[-1]))
    angle = positions.astype(jnp.float32)[:, None] * freq[None, :]
    cosine = jnp.cos(angle)[:, None, :]
    sine = jnp.sin(angle)[:, None, :]
    first = values[..., :half]
    second = values[..., half:]
    return jnp.concatenate([first * cosine - second * sine, second * cosine + first * sine], -1)

def attend(rows, sumsq, positions, sources, query_scale, key_scale):
    count = rows.shape[0]
    heads = query_scale.shape[0] // HD
    normed = rows.astype(jnp.float32) * lax.rsqrt(sumsq / D + eps)[:, None]
    query = rotate((normed * query_scale[None, :]).reshape(count, heads, HD), positions).astype(jnp.bfloat16)
    keys = rotate((normed * key_scale[None, :]).reshape(count, heads, HD), positions).astype(jnp.bfloat16)
    value = normed.reshape(count, heads, HD).astype(jnp.bfloat16)
    allowed = (sources[None, :] == sources[:, None]) & (positions[None, :] <= positions[:, None])
    scores = jnp.einsum('qhd,khd->hqk', query.astype(jnp.float32), keys.astype(jnp.float32)) / math.sqrt(HD)
    scores = jnp.where(allowed[None], scores, -1e+30)
    top = lax.optimization_barrier(jnp.max(scores, -1, keepdims=True))
    expd = jnp.exp(scores - top)
    weights = (expd / lax.optimization_barrier(jnp.sum(expd, -1, keepdims=True))).astype(jnp.bfloat16)
    out = jnp.einsum('hqk,khd->qhd', weights.astype(jnp.float32), value.astype(jnp.float32))
    return out.reshape(count, heads * HD).astype(jnp.bfloat16)

def reference(partials, kept_positions, destination, slot_index, query_scale, key_scale):

    def reduce_segment(piece):
        return lax.optimization_barrier(jnp.sum(piece.astype(jnp.float32), axis=0)).astype(jnp.bfloat16)
    hidden = lax.map(reduce_segment, partials)
    where_to = (destination.astype(jnp.int32) * KEPT + slot_index.astype(jnp.int32)).reshape(-1)
    packed = jnp.zeros((N_SECTION * KEPT, D), jnp.bfloat16).at[where_to].set(hidden.reshape(-1, D))
    packed_pos = jnp.zeros((N_SECTION * KEPT,), jnp.int32).at[where_to].set(kept_positions.reshape(-1).astype(jnp.int32))
    anchor = jnp.repeat(jnp.arange(N_SECTION, dtype=jnp.int32), KEPT)
    packed_src = jnp.zeros((N_SECTION * KEPT,), jnp.int32).at[where_to].set(anchor)

    def one_pack(items):
        rows, positions, sources = items
        sumsq = lax.optimization_barrier(jnp.sum(jnp.square(rows.astype(jnp.float32)), 1))
        return attend(rows, sumsq, positions, sources, query_scale, key_scale)
    out = lax.map(one_pack, (packed.reshape(N_SECTION, KEPT, D), packed_pos.reshape(N_SECTION, KEPT), packed_src.reshape(N_SECTION, KEPT)))
    return out.reshape(N_SECTION * KEPT, D)
```

```python
import functools
import math

import jax
import jax.numpy as jnp
import numpy as np
from jax import lax
from jax.experimental import pallas as pl
from jax.experimental.pallas import tpu as pltpu
from jax.sharding import PartitionSpec as P

HD = 128
CAP = 8
EPS = 1e-05
THETA = 500000.0
BLOCK = 128
PAIR = 2 * HD
MESH = pl.DeviceIdType.MESH


def link_load(offset):
    load = [0] * 6
    for axis, step in enumerate(offset):
        if step in (1, 2):
            load[2 * axis] += 1
        if step in (2, 3):
            load[2 * axis + 1] += 1
    return load


def offset_order(side):
    rest = [(a, b, c) for a in range(side) for b in range(side) for c in range(side)][1:]
    total = [0] * 6
    order = []
    while rest:
        def cost(offset):
            load = link_load(offset)
            after = [t + l for t, l in zip(total, load)]
            mean = sum(after) / 6
            return max(after) - min(after), sum((a - mean) ** 2 for a in after), -sum(load)

        best = min(rest, key=cost)
        rest.remove(best)
        total = [t + l for t, l in zip(total, link_load(best))]
        order.append(best)
    return order


def kernel(
    side, rows, width, pieces, early,
    part_ref, pos_ref, dest_ref, slot_ref, qscale_ref, kscale_ref, freq_ref,
    out_ref,
    own, recv, outbox, inbox, result, before_ref, gather_ref, scatter_ref, key_ref,
    posb, slotb, cos_ref, sin_ref, bias_ref, acc, half, half_in, total, total_in, inv_ref, att_ref, scale_ref,
    own_sem, xsend_sem, xrecv_sem, send_sem, recv_sem, hsend_sem, hrecv_sem, tsend_sem, trecv_sem, out_sem,
):
    f32, bf16 = jnp.float32, jnp.bfloat16
    segments = side ** 3
    step = width // pieces
    me = lax.axis_index("section")
    tp = lax.axis_index("tp")
    other = 1 - tp
    here = (me // (side * side), (me // side) % side, me % side)
    order = offset_order(side)

    def peer(offset):
        at = [lax.rem(h + o, side) for h, o in zip(here, offset)]
        return (at[0] * side + at[1]) * side + at[2]

    barrier = pltpu.get_barrier_semaphore()

    def own_copy(c):
        columns = pl.ds(pl.multiple_of(tp * width + c * step, HD), step)
        return pltpu.make_async_copy(part_ref.at[:, columns], own.at[c], own_sem.at[c])

    def exchange(c):
        columns = pl.ds(pl.multiple_of(other * width + c * step, HD), step)
        return pltpu.make_async_remote_copy(
            src_ref=part_ref.at[:, columns], dst_ref=recv.at[c],
            send_sem=xsend_sem.at[c], recv_sem=xrecv_sem.at[c],
            device_id=(me, other), device_id_type=MESH,
        )

    pl.semaphore_signal(barrier, inc=1, device_id=(me, other), device_id_type=MESH)
    for offset in order:
        pl.semaphore_signal(barrier, inc=1, device_id=(peer(offset), tp), device_id_type=MESH)
    for c in range(pieces):
        own_copy(c).start()

    before_ref[...] = (
        lax.broadcasted_iota(jnp.int32, (rows, rows), 0) < lax.broadcasted_iota(jnp.int32, (rows, rows), 1)
    ).astype(f32).astype(bf16)
    mine = dest_ref[pl.ds(me, 1), :]
    member = mine == lax.broadcasted_iota(jnp.int32, (segments, rows), 0)
    ahead = jnp.dot(member.astype(f32).astype(bf16), before_ref[...], preferred_element_type=f32)
    rank = jnp.sum(jnp.where(member, ahead, 0.0), axis=0, keepdims=True)
    target = mine * CAP + rank.astype(jnp.int32)
    gather_ref[...] = (
        lax.broadcasted_iota(jnp.int32, (rows, rows), 0) == target
    ).astype(f32).astype(bf16)
    acc[...] = jnp.zeros_like(acc)

    pl.semaphore_wait(barrier, segments)
    for c in range(pieces):
        exchange(c).start()

    def send_piece(c):
        for offset in order:
            there = peer(offset)
            pltpu.make_async_remote_copy(
                src_ref=outbox.at[c, there], dst_ref=inbox.at[c, me],
                send_sem=send_sem, recv_sem=recv_sem.at[c],
                device_id=(there, tp), device_id_type=MESH,
            ).start()

    def reduce_piece(c):
        own_copy(c).wait()
        exchange(c).wait_recv()

        def strip(i, carry):
            columns = pl.ds(pl.multiple_of(i * PAIR, PAIR), PAIR)
            summed = (own[c, :, columns].astype(f32) + recv[c, :, columns].astype(f32)).astype(bf16)
            moved = jnp.dot(gather_ref[...], summed, preferred_element_type=f32)
            outbox[c, :, :, columns] = moved.reshape(segments, CAP, PAIR).astype(bf16)
            square = moved * moved
            acc[...] += square[:, :HD] + square[:, HD:]
            return carry

        lax.fori_loop(0, step // PAIR, strip, 0)
        inbox[c, pl.ds(me, 1)] = outbox[c, pl.ds(me, 1)]

    def early_piece(c, carry):
        reduce_piece(c)
        send_piece(c)
        return carry

    lax.fori_loop(0, early, early_piece, 0)

    def late_piece(c, carry):
        reduce_piece(c)
        return carry

    lax.fori_loop(early, pieces, late_piece, 0)

    lane = lax.broadcasted_iota(jnp.int32, (CAP, HD), 1)
    diagonal = lane == lax.broadcasted_iota(jnp.int32, (CAP, HD), 0)

    def half_rows(i, carry):
        for u in range(8):
            s = i * 8 + u
            tile = acc[pl.ds(pl.multiple_of(s * CAP, CAP), CAP), :]
            column = jnp.sum(tile, axis=1, keepdims=True)
            half[s] = jnp.sum(jnp.where(diagonal, column, 0.0), axis=0, keepdims=True)
        return carry

    lax.fori_loop(0, segments // 8, half_rows, 0)
    halves = pltpu.make_async_remote_copy(
        src_ref=half, dst_ref=half_in, send_sem=hsend_sem, recv_sem=hrecv_sem,
        device_id=(me, other), device_id_type=MESH,
    )
    halves.start()

    arriving = dest_ref[...] == me
    ahead = jnp.dot(arriving.astype(f32).astype(bf16), before_ref[...], preferred_element_type=f32)
    key_ref[...] = jnp.where(arriving, ahead, -1.0)
    halves.wait()
    total[...] = half[...] + half_in[...]
    for offset in order:
        there = peer(offset)
        pltpu.make_async_remote_copy(
            src_ref=total.at[there], dst_ref=total_in.at[me], send_sem=tsend_sem, recv_sem=trecv_sem,
            device_id=(there, tp), device_id_type=MESH,
        ).start()
    total_in[pl.ds(me, 1)] = total[pl.ds(me, 1)]

    def late_send(c, carry):
        send_piece(c)
        return carry

    lax.fori_loop(early, pieces, late_send, 0)

    place = lax.broadcasted_iota(jnp.int32, (CAP, rows), 0).astype(f32)

    def columns_of(i, carry):
        for u in range(8):
            s = i * 8 + u
            found = key_ref[pl.ds(s, 1), :] == place
            at = pl.ds(pl.multiple_of(s * CAP, CAP), CAP)
            p = jnp.sum(jnp.where(found, pos_ref[pl.ds(s, 1), :].astype(f32), 0.0), axis=1, keepdims=True)
            posb[at, :] = jnp.broadcast_to(p, (CAP, HD))
            q = jnp.sum(jnp.where(found, slot_ref[pl.ds(s, 1), :].astype(f32), 0.0), axis=1, keepdims=True)
            slotb[at, :] = jnp.broadcast_to(q, (CAP, HD))
        return carry

    lax.fori_loop(0, segments // 8, columns_of, 0)

    row_in = lax.broadcasted_iota(jnp.int32, (BLOCK, BLOCK), 0)
    column_in = lax.broadcasted_iota(jnp.int32, (BLOCK, BLOCK), 1)
    same = (row_in // CAP) == (column_in // CAP)
    on_diagonal = row_in == column_in
    slots = lax.broadcasted_iota(jnp.int32, (rows, BLOCK), 0).astype(f32)
    half_sign = jnp.where(lax.broadcasted_iota(jnp.int32, (1, HD), 1) < HD // 2, -1.0, 1.0)

    def tables(b, carry):
        at = pl.ds(pl.multiple_of(b * BLOCK, BLOCK), BLOCK)
        p = posb[at, :]
        across = jnp.sum(jnp.where(on_diagonal, p, 0.0), axis=0, keepdims=True)
        bias_ref[at, :] = jnp.where(same & (across <= p), 0.0, -1e30)
        goes = jnp.sum(jnp.where(on_diagonal, slotb[at, :], 0.0), axis=0, keepdims=True)
        scatter_ref[:, at] = (slots == goes).astype(f32).astype(bf16)
        angle = p * freq_ref[...]
        cos_ref[at, :] = jnp.cos(angle)
        sin_ref[at, :] = jnp.sin(angle) * half_sign
        return carry

    lax.fori_loop(0, rows // BLOCK, tables, 0)
    scale_ref[0:1, :] = qscale_ref[...] * (math.log2(math.e) / math.sqrt(HD))
    scale_ref[1:2, :] = kscale_ref[...]

    every = pl.ds(0, segments - 1)
    pltpu.make_async_copy(total_in.at[every], total_in.at[every], trecv_sem).wait()
    whole = 1.0 / (2 * width)

    def inverse_rows(i, carry):
        for u in range(8):
            s = i * 8 + u
            column = jnp.sum(jnp.where(diagonal, total_in[s], 0.0), axis=1, keepdims=True)
            at = pl.ds(pl.multiple_of(s * CAP, CAP), CAP)
            inv_ref[at, :] = jnp.broadcast_to(lax.rsqrt(column * whole + EPS), (CAP, HD))
        return carry

    lax.fori_loop(0, segments // 8, inverse_rows, 0)

    ones = jnp.ones((BLOCK, HD), bf16)

    def out_copy(c):
        columns = pl.ds(pl.multiple_of(c * step, HD), step)
        return pltpu.make_async_copy(result.at[c], out_ref.at[:, columns], out_sem.at[c])

    def attend_piece(c, carry):
        pltpu.make_async_copy(inbox.at[c, every], inbox.at[c, every], recv_sem.at[c]).wait()

        def two_heads(i, carry):
            for u in range(2):
                local = pl.ds(pl.multiple_of(i * PAIR + u * HD, HD), HD)
                feature = pl.ds(pl.multiple_of(c * step + i * PAIR + u * HD, HD), HD)
                qs = scale_ref[0:1, feature]
                ks = scale_ref[1:2, feature]
                qr = pltpu.roll(qs, HD // 2, 1)
                kr = pltpu.roll(ks, HD // 2, 1)
                for b in range(rows // BLOCK):
                    at = pl.ds(b * BLOCK, BLOCK)
                    groups = pl.ds(b * (BLOCK // CAP), BLOCK // CAP)
                    x = inbox[c, groups, :, local].astype(f32).reshape(BLOCK, HD)
                    normed = x * inv_ref[at, :]
                    value = normed.astype(bf16)
                    straight = normed * cos_ref[at, :]
                    crossed = pltpu.roll(normed, HD // 2, 1) * sin_ref[at, :]
                    query = (straight * qs + crossed * qr).astype(bf16)
                    keys = (straight * ks + crossed * kr).astype(bf16)
                    scores = lax.dot_general(
                        query, keys, (((1,), (1,)), ((), ())), preferred_element_type=f32
                    ) + bias_ref[at, :]
                    top = jnp.max(scores, axis=1, keepdims=True)
                    weights = jnp.exp2(scores - top).astype(bf16)
                    both = jnp.dot(
                        weights, jnp.concatenate([value, ones], axis=1), preferred_element_type=f32
                    )
                    att_ref[at, u * HD:(u + 1) * HD] = (both[:, :HD] / both[:, HD:]).astype(bf16)
            placed = jnp.dot(scatter_ref[...], att_ref[...], preferred_element_type=f32)
            result[c, :, pl.ds(pl.multiple_of(i * PAIR, PAIR), PAIR)] = placed.astype(bf16)
            return carry

        lax.fori_loop(0, step // PAIR, two_heads, 0)
        out_copy(c).start()
        return carry

    lax.fori_loop(0, pieces, attend_piece, 0)

    for c in range(pieces):
        exchange(c).wait_send()
        out_copy(c).wait()
    sent = outbox.at[:, every]
    pltpu.make_async_copy(sent, sent, send_sem).wait()
    pltpu.make_async_copy(total.at[every], total.at[every], tsend_sem).wait()


def local(pieces, early, partials, kept_positions, destination, slot_index, query_scale, key_scale):
    f32, bf16 = jnp.float32, jnp.bfloat16
    rows, full = partials.shape[2:]
    width = full // 2
    step = width // pieces
    segments = destination.shape[0]
    side = round(segments ** (1 / 3))
    freq = np.exp(np.arange(HD // 2, dtype=np.float32) * np.float32(-2.0 * math.log(THETA) / HD))
    freq = jnp.asarray(np.concatenate([freq, freq])[None, :].astype(np.float32))
    vmem = pl.BlockSpec(memory_space=pltpu.VMEM)
    sem = pltpu.SemaphoreType.DMA
    return pl.pallas_call(
        functools.partial(kernel, side, rows, width, pieces, early),
        out_shape=jax.ShapeDtypeStruct((rows, width), bf16),
        in_specs=[pl.BlockSpec(memory_space=pl.ANY)] + [vmem] * 6,
        out_specs=pl.BlockSpec(memory_space=pl.ANY),
        scratch_shapes=[
            pltpu.VMEM((pieces, rows, step), bf16),
            pltpu.VMEM((pieces, rows, step), bf16),
            pltpu.VMEM((pieces, segments, CAP, step), bf16),
            pltpu.VMEM((pieces, segments, CAP, step), bf16),
            pltpu.VMEM((pieces, rows, step), bf16),
            pltpu.VMEM((rows, rows), bf16),
            pltpu.VMEM((rows, rows), bf16),
            pltpu.VMEM((rows, rows), bf16),
            pltpu.VMEM((segments, rows), f32),
            pltpu.VMEM((rows, HD), f32),
            pltpu.VMEM((rows, HD), f32),
            pltpu.VMEM((rows, HD), f32),
            pltpu.VMEM((rows, HD), f32),
            pltpu.VMEM((rows, BLOCK), f32),
            pltpu.VMEM((rows, HD), f32),
            pltpu.VMEM((segments, 1, HD), f32),
            pltpu.VMEM((segments, 1, HD), f32),
            pltpu.VMEM((segments, 1, HD), f32),
            pltpu.VMEM((segments, 1, HD), f32),
            pltpu.VMEM((rows, HD), f32),
            pltpu.VMEM((rows, PAIR), bf16),
            pltpu.VMEM((8, width), f32),
            sem((pieces,)), sem((pieces,)), sem((pieces,)),
            sem, sem((pieces,)),
            sem, sem, sem, sem,
            sem((pieces,)),
        ],
        compiler_params=pltpu.CompilerParams(
            collective_id=0, has_side_effects=True, vmem_limit_bytes=40 * 2**20
        ),
        name="handoff",
    )(
        partials.reshape(rows, full), kept_positions, destination, slot_index,
        query_scale[None, :], key_scale[None, :], freq,
    )


def solution(mesh):
    in_specs = (P("section", "tp", None, None), P(), P(), P(), P("tp"), P("tp"))
    return jax.shard_map(
        functools.partial(local, 4, 2), mesh=mesh, in_specs=in_specs,
        out_specs=P("section", "tp"), check_vma=False,
    )
```

```python
import functools
import math

import jax
import jax.numpy as jnp
import numpy as np
from jax import lax
from jax.experimental import pallas as pl
from jax.experimental.pallas import tpu as pltpu
from jax.sharding import PartitionSpec as P

HD = 128
CAP = 8
EPS = 1e-05
THETA = 500000.0
BLOCK = 128
HEADS = 4
UNIT = HEADS * HD
MESH = pl.DeviceIdType.MESH


def link_load(offset):
    load = [0] * 6
    for axis, step in enumerate(offset):
        if step in (1, 2):
            load[2 * axis] += 1
        if step in (2, 3):
            load[2 * axis + 1] += 1
    return load


def offset_order(side):
    rest = [(a, b, c) for a in range(side) for b in range(side) for c in range(side)][1:]
    total = [0] * 6
    order = []
    while rest:
        def cost(offset):
            load = link_load(offset)
            after = [t + l for t, l in zip(total, load)]
            mean = sum(after) / 6
            return max(after) - min(after), sum((a - mean) ** 2 for a in after), -sum(load)

        best = min(rest, key=cost)
        rest.remove(best)
        total = [t + l for t, l in zip(total, link_load(best))]
        order.append(best)
    return order


def kernel(
    side, rows, width,
    part_ref, pos_in, dest_in, slot_in, qscale_in, kscale_in, freq_in,
    out_ref,
    dest_ref, pos_ref, slot_ref, qscale_ref, kscale_ref, freq_ref,
    own, recv, outbox, inbox, before_ref, gather_ref, scatter_ref, key_ref,
    posb, slotb, cos_ref, sin_ref, bias_ref, acc, half, half_in, total, total_in, inv_ref, att_ref, scale_ref,
    own_sem, xsend_sem, xrecv_sem, send_sem, recv_sem, hsend_sem, hrecv_sem, tsend_sem, trecv_sem, load_sem,
):
    f32, bf16 = jnp.float32, jnp.bfloat16
    segments = side ** 3
    units = width // UNIT
    me = lax.axis_index("section")
    tp = lax.axis_index("tp")
    other = 1 - tp
    here = (me // (side * side), (me // side) % side, me % side)
    order = offset_order(side)

    def peer(offset):
        at = [lax.rem(h + o, side) for h, o in zip(here, offset)]
        return (at[0] * side + at[1]) * side + at[2]

    barrier = pltpu.get_barrier_semaphore()

    def own_copy(u):
        columns = pl.ds(pl.multiple_of(tp * width + u * UNIT, UNIT), UNIT)
        return pltpu.make_async_copy(part_ref.at[:, columns], own.at[u], own_sem.at[u])

    def exchange(u):
        columns = pl.ds(pl.multiple_of(other * width + u * UNIT, UNIT), UNIT)
        return pltpu.make_async_remote_copy(
            src_ref=part_ref.at[:, columns], dst_ref=recv.at[u],
            send_sem=xsend_sem.at[u], recv_sem=xrecv_sem.at[u],
            device_id=(me, other), device_id_type=MESH,
        )

    pl.semaphore_signal(barrier, inc=1, device_id=(me, other), device_id_type=MESH)
    for offset in order:
        pl.semaphore_signal(barrier, inc=1, device_id=(peer(offset), tp), device_id_type=MESH)
    loads = [
        pltpu.make_async_copy(source, place, load_sem.at[i])
        for i, (source, place) in enumerate((
            (dest_in, dest_ref), (pos_in, pos_ref), (slot_in, slot_ref),
            (qscale_in, qscale_ref), (kscale_in, kscale_ref), (freq_in, freq_ref),
        ))
    ]
    for load in loads:
        load.start()
    for u in range(units):
        own_copy(u).start()

    before_ref[...] = (
        lax.broadcasted_iota(jnp.int32, (rows, rows), 0) < lax.broadcasted_iota(jnp.int32, (rows, rows), 1)
    ).astype(f32).astype(bf16)
    loads[0].wait()
    mine = dest_ref[pl.ds(me, 1), :]
    member = mine == lax.broadcasted_iota(jnp.int32, (segments, rows), 0)
    ahead = jnp.dot(member.astype(f32).astype(bf16), before_ref[...], preferred_element_type=f32)
    rank = jnp.sum(jnp.where(member, ahead, 0.0), axis=0, keepdims=True)
    target = mine * CAP + rank.astype(jnp.int32)
    gather_ref[...] = (
        lax.broadcasted_iota(jnp.int32, (rows, rows), 0) == target
    ).astype(f32).astype(bf16)
    acc[...] = jnp.zeros_like(acc)

    pl.semaphore_wait(barrier, segments)
    for u in range(2):
        exchange(u).start()

    def send(first, count, piece):
        for offset in order:
            there = peer(offset)
            pltpu.make_async_remote_copy(
                src_ref=outbox.at[pl.ds(first, count), there], dst_ref=inbox.at[pl.ds(first, count), me],
                send_sem=send_sem, recv_sem=recv_sem.at[piece],
                device_id=(there, tp), device_id_type=MESH,
            ).start()

    def reduce_unit(u, carry):
        own_copy(u).wait()
        exchange(u).wait_recv()

        @pl.when(u + 2 < units)
        def _():
            exchange(u + 2).start()

        for i in range(HEADS // 2):
            columns = slice(2 * i * HD, 2 * (i + 1) * HD)
            summed = (own[u, :, columns].astype(f32) + recv[u, :, columns].astype(f32)).astype(bf16)
            moved = jnp.dot(gather_ref[...], summed, preferred_element_type=f32)
            outbox[u, :, :, columns] = moved.reshape(segments, CAP, 2 * HD).astype(bf16)
            square = moved * moved
            acc[...] += square[:, :HD] + square[:, HD:]
        inbox[u, pl.ds(me, 1)] = outbox[u, pl.ds(me, 1)]
        return carry

    lax.fori_loop(0, 1, reduce_unit, 0)
    send(0, 1, 0)
    lax.fori_loop(1, 3, reduce_unit, 0)
    send(1, 2, 1)
    lax.fori_loop(3, units, reduce_unit, 0)

    lane = lax.broadcasted_iota(jnp.int32, (CAP, HD), 1)
    diagonal = lane == lax.broadcasted_iota(jnp.int32, (CAP, HD), 0)

    def half_rows(i, carry):
        for u in range(8):
            s = i * 8 + u
            tile = acc[pl.ds(pl.multiple_of(s * CAP, CAP), CAP), :]
            column = jnp.sum(tile, axis=1, keepdims=True)
            half[s] = jnp.sum(jnp.where(diagonal, column, 0.0), axis=0, keepdims=True)
        return carry

    lax.fori_loop(0, segments // 8, half_rows, 0)
    halves = pltpu.make_async_remote_copy(
        src_ref=half, dst_ref=half_in, send_sem=hsend_sem, recv_sem=hrecv_sem,
        device_id=(me, other), device_id_type=MESH,
    )
    halves.start()

    arriving = dest_ref[...] == me
    ahead = jnp.dot(arriving.astype(f32).astype(bf16), before_ref[...], preferred_element_type=f32)
    key_ref[...] = jnp.where(arriving, ahead, -1.0)
    halves.wait()
    total[...] = half[...] + half_in[...]
    for offset in order:
        there = peer(offset)
        pltpu.make_async_remote_copy(
            src_ref=total.at[there], dst_ref=total_in.at[me], send_sem=tsend_sem, recv_sem=trecv_sem,
            device_id=(there, tp), device_id_type=MESH,
        ).start()
    total_in[pl.ds(me, 1)] = total[pl.ds(me, 1)]

    def send_middle(p, carry):
        send(2 * p - 1, 2, p)
        return carry

    lax.fori_loop(2, units // 2, send_middle, 0)
    send(units - 1, 1, units // 2)

    for load in loads[1:]:
        load.wait()
    place = lax.broadcasted_iota(jnp.int32, (CAP, rows), 0).astype(f32)

    def columns_of(i, carry):
        for u in range(8):
            s = i * 8 + u
            found = key_ref[pl.ds(s, 1), :] == place
            at = pl.ds(pl.multiple_of(s * CAP, CAP), CAP)
            p = jnp.sum(jnp.where(found, pos_ref[pl.ds(s, 1), :].astype(f32), 0.0), axis=1, keepdims=True)
            posb[at, :] = jnp.broadcast_to(p, (CAP, HD))
            q = jnp.sum(jnp.where(found, slot_ref[pl.ds(s, 1), :].astype(f32), 0.0), axis=1, keepdims=True)
            slotb[at, :] = jnp.broadcast_to(q, (CAP, HD))
        return carry

    lax.fori_loop(0, segments // 8, columns_of, 0)

    row_in = lax.broadcasted_iota(jnp.int32, (BLOCK, BLOCK), 0)
    column_in = lax.broadcasted_iota(jnp.int32, (BLOCK, BLOCK), 1)
    same = (row_in // CAP) == (column_in // CAP)
    on_diagonal = row_in == column_in
    slots = lax.broadcasted_iota(jnp.int32, (rows, BLOCK), 0).astype(f32)
    half_sign = jnp.where(lax.broadcasted_iota(jnp.int32, (1, HD), 1) < HD // 2, -1.0, 1.0)

    def tables(b, carry):
        at = pl.ds(pl.multiple_of(b * BLOCK, BLOCK), BLOCK)
        p = posb[at, :]
        across = jnp.sum(jnp.where(on_diagonal, p, 0.0), axis=0, keepdims=True)
        bias_ref[at, :] = jnp.where(same & (across <= p), 0.0, -1e30)
        goes = jnp.sum(jnp.where(on_diagonal, slotb[at, :], 0.0), axis=0, keepdims=True)
        scatter_ref[:, at] = (slots == goes).astype(f32).astype(bf16)
        angle = p * freq_ref[...]
        cos_ref[at, :] = jnp.cos(angle)
        sin_ref[at, :] = jnp.sin(angle) * half_sign
        return carry

    lax.fori_loop(0, rows // BLOCK, tables, 0)
    scale_ref[0:1, :] = qscale_ref[...] * (math.log2(math.e) / math.sqrt(HD))
    scale_ref[1:2, :] = kscale_ref[...]

    every = pl.ds(0, segments - 1)
    pltpu.make_async_copy(total_in.at[every], total_in.at[every], trecv_sem).wait()
    whole = 1.0 / (2 * width)

    def inverse_rows(i, carry):
        for u in range(8):
            s = i * 8 + u
            column = jnp.sum(jnp.where(diagonal, total_in[s], 0.0), axis=1, keepdims=True)
            at = pl.ds(pl.multiple_of(s * CAP, CAP), CAP)
            inv_ref[at, :] = jnp.broadcast_to(lax.rsqrt(column * whole + EPS), (CAP, HD))
        return carry

    lax.fori_loop(0, segments // 8, inverse_rows, 0)

    ones = jnp.ones((BLOCK, HD), bf16)

    def arrived(first, count, piece):
        at = inbox.at[pl.ds(first, count), every]
        pltpu.make_async_copy(at, at, recv_sem.at[piece]).wait()

    def attend_unit(unit, carry):
        @pl.when(unit == 0)
        def _():
            arrived(0, 1, 0)

        @pl.when((unit % 2 == 1) & (unit < units - 1))
        def _():
            arrived(unit, 2, (unit + 1) // 2)

        @pl.when(unit == units - 1)
        def _():
            arrived(units - 1, 1, units // 2)

        tiles = []
        for h in range(HEADS):
            local = slice(h * HD, (h + 1) * HD)
            feature = pl.ds(pl.multiple_of(unit * UNIT + h * HD, HD), HD)
            qs = scale_ref[0:1, feature]
            ks = scale_ref[1:2, feature]
            qr = pltpu.roll(qs, HD // 2, 1)
            kr = pltpu.roll(ks, HD // 2, 1)
            for b in range(rows // BLOCK):
                at = slice(b * BLOCK, (b + 1) * BLOCK)
                groups = slice(b * (BLOCK // CAP), (b + 1) * (BLOCK // CAP))
                x = inbox[unit, groups, :, local].astype(f32).reshape(BLOCK, HD)
                normed = x * inv_ref[at, :]
                straight = normed * cos_ref[at, :]
                crossed = pltpu.roll(normed, HD // 2, 1) * sin_ref[at, :]
                query = (straight * qs + crossed * qr).astype(bf16)
                keys = (straight * ks + crossed * kr).astype(bf16)
                tiles.append((at, local, query, keys, normed.astype(bf16)))
        scores = [
            lax.dot_general(query, keys, (((1,), (1,)), ((), ())), preferred_element_type=f32)
            for _, _, query, keys, _ in tiles
        ]
        weights = []
        for (at, *_), score in zip(tiles, scores):
            score = score + bias_ref[at, :]
            top = jnp.max(score, axis=1, keepdims=True)
            weights.append(jnp.exp2(score - top).astype(bf16))
        sums = [
            jnp.dot(weight, jnp.concatenate([value, ones], axis=1), preferred_element_type=f32)
            for (*_, value), weight in zip(tiles, weights)
        ]
        for (at, local, *_), both in zip(tiles, sums):
            att_ref[at, local] = (both[:, :HD] / both[:, HD:]).astype(bf16)
        placed = jnp.dot(scatter_ref[...], att_ref[...], preferred_element_type=f32)
        out_ref[:, pl.ds(pl.multiple_of(unit * UNIT, UNIT), UNIT)] = placed.astype(bf16)
        return carry

    lax.fori_loop(0, units, attend_unit, 0)

    for u in range(units):
        exchange(u).wait_send()
    sent = outbox.at[:, every]
    pltpu.make_async_copy(sent, sent, send_sem).wait()
    pltpu.make_async_copy(total.at[every], total.at[every], tsend_sem).wait()


def local(partials, kept_positions, destination, slot_index, query_scale, key_scale):
    f32, bf16 = jnp.float32, jnp.bfloat16
    rows, full = partials.shape[2:]
    width = full // 2
    units = width // UNIT
    segments = destination.shape[0]
    side = round(segments ** (1 / 3))
    freq = np.exp(np.arange(HD // 2, dtype=np.float32) * np.float32(-2.0 * math.log(THETA) / HD))
    freq = jnp.asarray(np.concatenate([freq, freq])[None, :].astype(np.float32))
    vmem = pl.BlockSpec(memory_space=pltpu.VMEM)
    sem = pltpu.SemaphoreType.DMA
    return pl.pallas_call(
        functools.partial(kernel, side, rows, width),
        out_shape=pltpu.VMEM((rows, width), bf16),
        in_specs=[pl.BlockSpec(memory_space=pltpu.HBM)] * 7,
        out_specs=vmem,
        scratch_shapes=[
            pltpu.VMEM(destination.shape, jnp.int32),
            pltpu.VMEM(destination.shape, jnp.int32),
            pltpu.VMEM(destination.shape, jnp.int32),
            pltpu.VMEM((1, width), f32),
            pltpu.VMEM((1, width), f32),
            pltpu.VMEM((1, HD), f32),
            pltpu.VMEM((units, rows, UNIT), bf16),
            pltpu.VMEM((units, rows, UNIT), bf16),
            pltpu.VMEM((units, segments, CAP, UNIT), bf16),
            pltpu.VMEM((units, segments, CAP, UNIT), bf16),
            pltpu.VMEM((rows, rows), bf16),
            pltpu.VMEM((rows, rows), bf16),
            pltpu.VMEM((rows, rows), bf16),
            pltpu.VMEM((segments, rows), f32),
            pltpu.VMEM((rows, HD), f32),
            pltpu.VMEM((rows, HD), f32),
            pltpu.VMEM((rows, HD), f32),
            pltpu.VMEM((rows, HD), f32),
            pltpu.VMEM((rows, BLOCK), f32),
            pltpu.VMEM((rows, HD), f32),
            pltpu.VMEM((segments, 1, HD), f32),
            pltpu.VMEM((segments, 1, HD), f32),
            pltpu.VMEM((segments, 1, HD), f32),
            pltpu.VMEM((segments, 1, HD), f32),
            pltpu.VMEM((rows, HD), f32),
            pltpu.VMEM((rows, UNIT), bf16),
            pltpu.VMEM((8, width), f32),
            sem((units,)), sem((units,)), sem((units,)),
            sem, sem((units // 2 + 1,)),
            sem, sem, sem, sem,
            sem((6,)),
        ],
        compiler_params=pltpu.CompilerParams(
            collective_id=0, has_side_effects=True, vmem_limit_bytes=40 * 2**20
        ),
        name="handoff",
    )(*(
        pltpu.with_memory_space_constraint(array, pltpu.HBM)
        for array in (
            partials.reshape(rows, full), kept_positions, destination, slot_index,
            query_scale[None, :], key_scale[None, :], freq,
        )
    ))


def solution(mesh):
    in_specs = (P("section", "tp", None, None), P(), P(), P(), P("tp"), P("tp"))
    return jax.shard_map(
        local, mesh=mesh, in_specs=in_specs,
        out_specs=P("section", "tp"), check_vma=False,
    )
```

```python
import functools
import math

import jax
import jax.numpy as jnp
import numpy as np
from jax import lax
from jax.experimental import pallas as pl
from jax.experimental.pallas import tpu as pltpu
from jax.sharding import PartitionSpec as P

HD = 128
CAP = 8
EPS = 1e-05
THETA = 500000.0
BLOCK = 128
HEADS = 4
UNIT = HEADS * HD
STRIP = UNIT // 2
MESH = pl.DeviceIdType.MESH


def attend(load, store, inv_ref, cos_ref, sin_ref, bias_ref, scale_ref, first):
    f32, bf16 = jnp.float32, jnp.bfloat16
    rows = inv_ref.shape[0]
    ones = jnp.ones((BLOCK, HD), bf16)
    tiles = []
    for h in range(HEADS):
        local = slice(h * HD, (h + 1) * HD)
        feature = pl.ds(pl.multiple_of(first + h * HD, HD), HD)
        qs = scale_ref[0:1, feature]
        ks = scale_ref[1:2, feature]
        qr = pltpu.roll(qs, HD // 2, 1)
        kr = pltpu.roll(ks, HD // 2, 1)
        for b in range(rows // BLOCK):
            at = slice(b * BLOCK, (b + 1) * BLOCK)
            groups = slice(b * (BLOCK // CAP), (b + 1) * (BLOCK // CAP))
            x = load(groups, local).astype(f32).reshape(BLOCK, HD)
            normed = x * inv_ref[at, :]
            straight = normed * cos_ref[at, :]
            crossed = pltpu.roll(normed, HD // 2, 1) * sin_ref[at, :]
            query = (straight * qs + crossed * qr).astype(bf16)
            keys = (straight * ks + crossed * kr).astype(bf16)
            tiles.append((at, groups, local, query, keys, normed.astype(bf16)))
    scores = [
        lax.dot_general(query, keys, (((1,), (1,)), ((), ())), preferred_element_type=f32)
        for _, _, _, query, keys, _ in tiles
    ]
    weights = []
    for (at, *_), score in zip(tiles, scores):
        score = score + bias_ref[at, :]
        top = jnp.max(score, axis=1, keepdims=True)
        weights.append(jnp.exp2(score - top).astype(bf16))
    sums = [
        jnp.dot(weight, jnp.concatenate([value, ones], axis=1), preferred_element_type=f32)
        for (*_, value), weight in zip(tiles, weights)
    ]
    for (at, groups, local, *_), both in zip(tiles, sums):
        store(at, groups, local, both[:, :HD] / both[:, HD:])


def link_load(offset):
    load = [0] * 6
    for axis, step in enumerate(offset):
        if step in (1, 2):
            load[2 * axis] += 1
        if step in (2, 3):
            load[2 * axis + 1] += 1
    return load


def offset_order(side):
    rest = [(a, b, c) for a in range(side) for b in range(side) for c in range(side)][1:]
    total = [0] * 6
    order = []
    while rest:
        def cost(offset):
            load = link_load(offset)
            after = [t + l for t, l in zip(total, load)]
            mean = sum(after) / 6
            return max(after) - min(after), sum((a - mean) ** 2 for a in after), -sum(load)

        best = min(rest, key=cost)
        rest.remove(best)
        total = [t + l for t, l in zip(total, link_load(best))]
        order.append(best)
    return order


def kernel(
    side, rows, width,
    part_ref, pos_in, dest_in, slot_in, qscale_in, kscale_in, freq_in,
    placed_ref, last_ref, scatter_ref,
    dest_ref, pos_ref, slot_ref, qscale_ref, kscale_ref, freq_ref,
    own, recv, outbox, inbox, before_ref, gather_ref, key_ref,
    inv_ref, cos_ref, sin_ref, bias_ref, scale_ref,
    posb, slotb, acc, half, half_in, total, total_in, att_ref,
    own_sem, xsend_sem, xrecv_sem, send_sem, recv_sem, hsend_sem, hrecv_sem, tsend_sem, trecv_sem, load_sem,
):
    f32, bf16 = jnp.float32, jnp.bfloat16
    segments = side ** 3
    units = width // UNIT
    me = lax.axis_index("section")
    tp = lax.axis_index("tp")
    other = 1 - tp
    strips = width // STRIP
    z, y, x = me // (side * side), lax.rem(me // side, side), lax.rem(me, side)

    order = offset_order(side)

    def each_peer(act):
        for offset in order:
            at = [lax.rem(h + o, side) for h, o in zip((z, y, x), offset)]
            act((at[0] * side + at[1]) * side + at[2])

    barrier = pltpu.get_barrier_semaphore()

    def own_copy(u):
        columns = pl.ds(pl.multiple_of(tp * width + u * STRIP, STRIP), STRIP)
        return pltpu.make_async_copy(part_ref.at[:, columns], own.at[u], own_sem.at[u])

    def exchange(u):
        columns = pl.ds(pl.multiple_of(other * width + u * STRIP, STRIP), STRIP)
        return pltpu.make_async_remote_copy(
            src_ref=part_ref.at[:, columns], dst_ref=recv.at[u],
            send_sem=xsend_sem.at[u], recv_sem=xrecv_sem.at[u],
            device_id=(me, other), device_id_type=MESH,
        )

    pl.semaphore_signal(barrier, inc=1, device_id=(me, other), device_id_type=MESH)
    each_peer(lambda there: pl.semaphore_signal(barrier, inc=1, device_id=(there, tp), device_id_type=MESH))
    loads = [
        pltpu.make_async_copy(source, place, load_sem.at[i])
        for i, (source, place) in enumerate((
            (dest_in, dest_ref), (pos_in, pos_ref), (slot_in, slot_ref),
            (qscale_in, qscale_ref), (kscale_in, kscale_ref), (freq_in, freq_ref),
        ))
    ]
    for load in loads:
        load.start()
    for u in range(strips):
        own_copy(u).start()

    before_ref[...] = (
        lax.broadcasted_iota(jnp.int32, (rows, rows), 0) < lax.broadcasted_iota(jnp.int32, (rows, rows), 1)
    ).astype(f32).astype(bf16)
    loads[0].wait()
    mine = dest_ref[pl.ds(me, 1), :]
    member = mine == lax.broadcasted_iota(jnp.int32, (segments, rows), 0)
    ahead = jnp.dot(member.astype(f32).astype(bf16), before_ref[...], preferred_element_type=f32)
    rank = jnp.sum(jnp.where(member, ahead, 0.0), axis=0, keepdims=True)
    target = mine * CAP + rank.astype(jnp.int32)
    gather_ref[...] = (
        lax.broadcasted_iota(jnp.int32, (rows, rows), 0) == target
    ).astype(f32).astype(bf16)
    acc[...] = jnp.zeros_like(acc)

    pl.semaphore_wait(barrier, segments)
    for u in range(2):
        exchange(u).start()

    def send(source, target, piece):
        def one(there):
            pltpu.make_async_remote_copy(
                src_ref=source(there), dst_ref=target, send_sem=send_sem, recv_sem=recv_sem.at[piece],
                device_id=(there, tp), device_id_type=MESH,
            ).start()

        each_peer(one)

    def send_half(i):
        columns = pl.ds(i * STRIP, STRIP)
        send(lambda there: outbox.at[0, there, :, columns], inbox.at[0, me, :, columns], i)

    def send_pair(p, carry):
        two = pl.ds(2 * p - 3, 2)
        send(lambda there: outbox.at[two, there], inbox.at[two, me], p)
        return carry

    def reduce_strip(u, carry):
        own_copy(u).wait()
        exchange(u).wait_recv()

        @pl.when(u + 2 < strips)
        def _():
            exchange(u + 2).start()

        unit = u // 2
        columns = pl.ds(pl.multiple_of(lax.rem(u, 2) * STRIP, STRIP), STRIP)
        summed = (own[u].astype(f32) + recv[u].astype(f32)).astype(bf16)
        moved = jnp.dot(gather_ref[...], summed, preferred_element_type=f32)
        outbox[unit, :, :, columns] = moved.reshape(segments, CAP, STRIP).astype(bf16)
        square = moved * moved
        acc[...] += square[:, :HD] + square[:, HD:]
        return carry

    lax.fori_loop(0, 1, reduce_strip, 0)
    send_half(0)
    lax.fori_loop(1, 2, reduce_strip, 0)
    send_half(1)
    lax.fori_loop(2, 6, reduce_strip, 0)
    send_pair(2, 0)
    lax.fori_loop(6, 10, reduce_strip, 0)
    send_pair(3,0)
    lax.fori_loop(10, strips, reduce_strip, 0)
    mine_too = pl.ds(me, 1)
    inbox[:, mine_too] = outbox[pl.ds(0, units - 1), mine_too]

    lane = lax.broadcasted_iota(jnp.int32, (CAP, HD), 1)
    diagonal = lane == lax.broadcasted_iota(jnp.int32, (CAP, HD), 0)

    def half_rows(i, carry):
        for u in range(8):
            s = i * 8 + u
            tile = acc[pl.ds(pl.multiple_of(s * CAP, CAP), CAP), :]
            column = jnp.sum(tile, axis=1, keepdims=True)
            half[s] = jnp.sum(jnp.where(diagonal, column, 0.0), axis=0, keepdims=True)
        return carry

    lax.fori_loop(0, segments // 8, half_rows, 0)
    halves = pltpu.make_async_remote_copy(
        src_ref=half, dst_ref=half_in, send_sem=hsend_sem, recv_sem=hrecv_sem,
        device_id=(me, other), device_id_type=MESH,
    )
    halves.start()

    arriving = dest_ref[...] == me
    ahead = jnp.dot(arriving.astype(f32).astype(bf16), before_ref[...], preferred_element_type=f32)
    key_ref[...] = jnp.where(arriving, ahead, -1.0)
    halves.wait()
    total[...] = half[...] + half_in[...]

    def send_total(there):
        pltpu.make_async_remote_copy(
            src_ref=total.at[there], dst_ref=total_in.at[me], send_sem=tsend_sem, recv_sem=trecv_sem,
            device_id=(there, tp), device_id_type=MESH,
        ).start()

    each_peer(send_total)
    total_in[pl.ds(me, 1)] = total[pl.ds(me, 1)]

    pairs = units // 2 + 1
    lax.fori_loop(4, pairs, send_pair, 0)

    for load in loads[1:]:
        load.wait()
    scale_ref[0:1, :] = qscale_ref[...] * (math.log2(math.e) / math.sqrt(HD))
    scale_ref[1:2, :] = kscale_ref[...]
    place = lax.broadcasted_iota(jnp.int32, (CAP, rows), 0).astype(f32)
    row_in = lax.broadcasted_iota(jnp.int32, (BLOCK, BLOCK), 0)
    column_in = lax.broadcasted_iota(jnp.int32, (BLOCK, BLOCK), 1)
    same = (row_in // CAP) == (column_in // CAP)
    on_diagonal = row_in == column_in
    half_sign = jnp.where(lax.broadcasted_iota(jnp.int32, (1, HD), 1) < HD // 2, -1.0, 1.0)
    whole = 1.0 / (2 * width)

    def spread(found, row):
        column = jnp.sum(jnp.where(found, row.astype(f32), 0.0), axis=1, keepdims=True)
        return jnp.broadcast_to(column, (CAP, HD))

    def tables(b, carry):
        at = pl.ds(pl.multiple_of(b * BLOCK, BLOCK), BLOCK)
        p = posb[at, :]
        across = jnp.sum(jnp.where(on_diagonal, p, 0.0), axis=0, keepdims=True)
        bias_ref[at, :] = jnp.where(same & (across <= p), 0.0, -1e30)
        angle = p * freq_ref[...]
        cos_ref[at, :] = jnp.cos(angle)
        sin_ref[at, :] = jnp.sin(angle) * half_sign
        return carry

    def inverse_rows(sums):
        def some(i, carry):
            for u in range(8):
                s = i * 8 + u
                column = jnp.sum(jnp.where(diagonal, sums[s], 0.0), axis=1, keepdims=True)
                at = pl.ds(pl.multiple_of(s * CAP, CAP), CAP)
                inv_ref[at, :] = jnp.broadcast_to(lax.rsqrt(column * whole + EPS), (CAP, HD))
            return carry

        lax.fori_loop(0, segments // 8, some, 0)

    leaving = target.astype(f32)
    leaving_pos = pos_ref[pl.ds(me, 1), :]

    def leaving_columns(i, carry):
        for u in range(8):
            s = i * 8 + u
            found = leaving == place + (s * CAP).astype(f32)
            posb[pl.ds(pl.multiple_of(s * CAP, CAP), CAP), :] = spread(found, leaving_pos)
        return carry

    lax.fori_loop(0, segments // 8, leaving_columns, 0)
    lax.fori_loop(0, rows // BLOCK, tables, 0)
    inverse_rows(total)
    last = units - 1

    def store_leaving(at, groups, local, value):
        outbox[last, groups, :, local] = value.reshape(BLOCK // CAP, CAP, HD).astype(bf16)

    attend(
        lambda groups, local: outbox[last, groups, :, local], store_leaving,
        inv_ref, cos_ref, sin_ref, bias_ref, scale_ref, last * UNIT,
    )
    send(lambda there: outbox.at[last, there], last_ref.at[me], pairs)
    last_ref[mine_too] = outbox[last, mine_too]

    def columns_of(i, carry):
        for u in range(8):
            s = i * 8 + u
            found = key_ref[pl.ds(s, 1), :] == place
            at = pl.ds(pl.multiple_of(s * CAP, CAP), CAP)
            posb[at, :] = spread(found, pos_ref[pl.ds(s, 1), :])
            slotb[at, :] = spread(found, slot_ref[pl.ds(s, 1), :])
        return carry

    lax.fori_loop(0, segments // 8, columns_of, 0)
    lax.fori_loop(0, rows // BLOCK, tables, 0)
    slots = lax.broadcasted_iota(jnp.int32, (rows, BLOCK), 0).astype(f32)

    def scatter_block(b, carry):
        at = pl.ds(pl.multiple_of(b * BLOCK, BLOCK), BLOCK)
        goes = jnp.sum(jnp.where(on_diagonal, slotb[at, :], 0.0), axis=0, keepdims=True)
        scatter_ref[:, at] = (slots == goes).astype(f32).astype(bf16)
        return carry

    lax.fori_loop(0, rows // BLOCK, scatter_block, 0)

    every = pl.ds(0, segments - 1)
    pltpu.make_async_copy(total_in.at[every], total_in.at[every], trecv_sem).wait()
    inverse_rows(total_in)

    def arrived(at, piece):
        pltpu.make_async_copy(at, at, recv_sem.at[piece]).wait()

    def attend_unit(unit, carry):
        @pl.when(unit == 0)
        def _():
            arrived(inbox.at[0, every, :, pl.ds(0, STRIP)], 0)
            arrived(inbox.at[0, every, :, pl.ds(STRIP, STRIP)], 1)

        @pl.when(lax.rem(unit, 2) == 1)
        def _():
            arrived(inbox.at[pl.ds(unit, 2), every], (unit + 3) // 2)

        def store_arrived(at, groups, local, value):
            att_ref[at, local] = value.astype(bf16)

        first = unit * UNIT
        attend(
            lambda groups, local: inbox[unit, groups, :, local], store_arrived,
            inv_ref, cos_ref, sin_ref, bias_ref, scale_ref, first,
        )
        placed_ref[:, pl.ds(pl.multiple_of(first, UNIT), UNIT)] = jnp.dot(
            scatter_ref[...], att_ref[...], preferred_element_type=f32
        ).astype(bf16)
        return carry

    lax.fori_loop(0, units - 1, attend_unit, 0)
    arrived(last_ref.at[every], pairs)

    for u in range(strips):
        exchange(u).wait_send()
    sent = outbox.at[:, every]
    pltpu.make_async_copy(sent, sent, send_sem).wait()
    pltpu.make_async_copy(total.at[every], total.at[every], tsend_sem).wait()


def finish(placed_ref, last_ref, scatter_ref, out_ref, tail_ref, copy_sem):
    rows, width = placed_ref.shape
    done = width - UNIT
    early = pltpu.make_async_copy(
        placed_ref.at[:, pl.ds(0, done)], out_ref.at[:, pl.ds(0, done)], copy_sem.at[0]
    )
    early.start()
    arrived = last_ref[...].astype(jnp.float32).reshape(rows, UNIT).astype(jnp.bfloat16)
    tail_ref[...] = jnp.dot(
        scatter_ref[...], arrived, preferred_element_type=jnp.float32
    ).astype(jnp.bfloat16)
    late = pltpu.make_async_copy(tail_ref, out_ref.at[:, pl.ds(done, UNIT)], copy_sem.at[1])
    late.start()
    early.wait()
    late.wait()


def local(partials, kept_positions, destination, slot_index, query_scale, key_scale):
    f32, bf16 = jnp.float32, jnp.bfloat16
    rows, full = partials.shape[2:]
    width = full // 2
    units = width // UNIT
    segments = destination.shape[0]
    side = round(segments ** (1 / 3))
    freq = np.exp(np.arange(HD // 2, dtype=np.float32) * np.float32(-2.0 * math.log(THETA) / HD))
    freq = jnp.asarray(np.concatenate([freq, freq])[None, :].astype(np.float32))
    vmem = pl.BlockSpec(memory_space=pltpu.VMEM)
    hbm = pl.BlockSpec(memory_space=pltpu.HBM)
    sem = pltpu.SemaphoreType.DMA
    strips = 2 * units
    ints = pltpu.VMEM(destination.shape, jnp.int32)
    table = pltpu.VMEM((rows, HD), f32)
    square = pltpu.VMEM((rows, rows), bf16)
    sums = pltpu.VMEM((segments, 1, HD), f32)
    parts = pl.pallas_call(
        functools.partial(kernel, side, rows, width),
        out_shape=[
            pltpu.VMEM((rows, width), bf16),
            pltpu.VMEM((segments, CAP, UNIT), bf16),
            square,
        ],
        in_specs=[hbm] * 7,
        out_specs=[vmem] * 3,
        scratch_shapes=[
            ints, ints, ints,
            pltpu.VMEM((1, width), f32),
            pltpu.VMEM((1, width), f32),
            pltpu.VMEM((1, HD), f32),
            pltpu.VMEM((strips, rows, STRIP), bf16),
            pltpu.VMEM((strips, rows, STRIP), bf16),
            pltpu.VMEM((units, segments, CAP, UNIT), bf16),
            pltpu.VMEM((units - 1, segments, CAP, UNIT), bf16),
            square, square,
            pltpu.VMEM((segments, rows), f32),
            table, table, table, pltpu.VMEM((rows, BLOCK), f32),
            pltpu.VMEM((8, width), f32),
            table, table, table,
            sums, sums, sums, sums,
            pltpu.VMEM((rows, UNIT), bf16),
            sem((strips,)), sem((strips,)), sem((strips,)),
            sem, sem((units // 2 + 2,)),
            sem, sem, sem, sem,
            sem((6,)),
        ],
        compiler_params=pltpu.CompilerParams(
            collective_id=0, has_side_effects=True, vmem_limit_bytes=36 * 2**20
        ),
        name="handoff",
    )(*(
        pltpu.with_memory_space_constraint(array, pltpu.HBM)
        for array in (
            partials.reshape(rows, full), kept_positions, destination, slot_index,
            query_scale[None, :], key_scale[None, :], freq,
        )
    ))
    return pl.pallas_call(
        finish,
        out_shape=jax.ShapeDtypeStruct((rows, width), bf16),
        in_specs=[vmem] * 3,
        out_specs=pl.BlockSpec(memory_space=pl.ANY),
        scratch_shapes=[
            pltpu.VMEM((rows, UNIT), bf16),
            sem((2,)),
        ],
        compiler_params=pltpu.CompilerParams(vmem_limit_bytes=16 * 2**20),
        name="finish",
    )(*(pltpu.with_memory_space_constraint(part, pltpu.VMEM) for part in parts))


def solution(mesh):
    in_specs = (P("section", "tp", None, None), P(), P(), P(), P("tp"), P("tp"))
    return jax.shard_map(
        local, mesh=mesh, in_specs=in_specs,
        out_specs=P("section", "tp"), check_vma=False,
    )
```

```python
import functools
import math

import jax
import jax.numpy as jnp
import numpy as np
from jax import lax
from jax.experimental import pallas as pl
from jax.experimental.pallas import tpu as pltpu
from jax.sharding import PartitionSpec as P

HD = 128
CAP = 8
EPS = 1e-05
THETA = 500000.0
BLOCK = 128
HEADS = 4
UNIT = HEADS * HD
STRIP = UNIT // 2
MESH = pl.DeviceIdType.MESH


def attend(load, store, inv_ref, cos_ref, sin_ref, bias_ref, scale_ref, first):
    f32, bf16 = jnp.float32, jnp.bfloat16
    rows = inv_ref.shape[0]
    ones = jnp.ones((BLOCK, HD), bf16)
    tiles = []
    for h in range(HEADS):
        local = slice(h * HD, (h + 1) * HD)
        feature = pl.ds(pl.multiple_of(first + h * HD, HD), HD)
        qs = scale_ref[0:1, feature]
        ks = scale_ref[1:2, feature]
        qr = pltpu.roll(qs, HD // 2, 1)
        kr = pltpu.roll(ks, HD // 2, 1)
        for b in range(rows // BLOCK):
            at = slice(b * BLOCK, (b + 1) * BLOCK)
            groups = slice(b * (BLOCK // CAP), (b + 1) * (BLOCK // CAP))
            x = load(groups, local).astype(f32).reshape(BLOCK, HD)
            normed = x * inv_ref[at, :]
            straight = normed * cos_ref[at, :]
            crossed = pltpu.roll(normed, HD // 2, 1) * sin_ref[at, :]
            query = (straight * qs + crossed * qr).astype(bf16)
            keys = (straight * ks + crossed * kr).astype(bf16)
            tiles.append((at, groups, local, query, keys, normed.astype(bf16)))
    scores = [
        lax.dot_general(query, keys, (((1,), (1,)), ((), ())), preferred_element_type=f32)
        for _, _, _, query, keys, _ in tiles
    ]
    weights = []
    for (at, *_), score in zip(tiles, scores):
        score = score + bias_ref[at, :]
        top = jnp.max(score, axis=1, keepdims=True)
        weights.append(jnp.exp2(score - top).astype(bf16))
    sums = [
        jnp.dot(weight, jnp.concatenate([value, ones], axis=1), preferred_element_type=f32)
        for (*_, value), weight in zip(tiles, weights)
    ]
    for (at, groups, local, *_), both in zip(tiles, sums):
        store(at, groups, local, both[:, :HD] / both[:, HD:])


def link_load(offset):
    load = [0] * 6
    for axis, step in enumerate(offset):
        if step in (1, 2):
            load[2 * axis] += 1
        if step in (2, 3):
            load[2 * axis + 1] += 1
    return load


def offset_order(side):
    rest = [(a, b, c) for a in range(side) for b in range(side) for c in range(side)][1:]
    total = [0] * 6
    order = []
    while rest:
        def cost(offset):
            load = link_load(offset)
            after = [t + l for t, l in zip(total, load)]
            mean = sum(after) / 6
            return max(after) - min(after), sum((a - mean) ** 2 for a in after), -sum(load)

        best = min(rest, key=cost)
        rest.remove(best)
        total = [t + l for t, l in zip(total, link_load(best))]
        order.append(best)
    return order


def kernel(
    side, rows, width,
    part_ref, pos_in, dest_in, slot_in, qscale_in, kscale_in, freq_in,
    placed_ref, last_ref, scatter_ref,
    dest_ref, pos_ref, slot_ref, qscale_ref, kscale_ref, freq_ref,
    near, raw_out, raw_in, raw_other,
    own, recv, outbox, inbox, before_ref, gather_ref, key_ref,
    inv_ref, cos_ref, sin_ref, bias_ref, scale_ref,
    posb, slotb, acc, half, half_in, total, total_in, att_ref,
    own_sem, xsend_sem, xrecv_sem, send_sem, recv_sem, hsend_sem, hrecv_sem, tsend_sem, trecv_sem, load_sem,
    near_sem, raw_send_sem, raw_recv_sem, swap_send_sem, swap_recv_sem,
):
    f32, bf16 = jnp.float32, jnp.bfloat16
    segments = side ** 3
    units = width // UNIT
    me = lax.axis_index("section")
    tp = lax.axis_index("tp")
    other = 1 - tp
    strips = width // STRIP
    z, y, x = me // (side * side), lax.rem(me // side, side), lax.rem(me, side)

    order = offset_order(side)

    def each_peer(act):
        for offset in order:
            at = [lax.rem(h + side + o + tp * (side - 2 * o), side) for h, o in zip((z, y, x), offset)]
            act((at[0] * side + at[1]) * side + at[2])

    barrier = pltpu.get_barrier_semaphore()

    def own_copy(u):
        columns = pl.ds(pl.multiple_of(tp * width + u * STRIP, STRIP), STRIP)
        return pltpu.make_async_copy(part_ref.at[:, columns], own.at[u], own_sem.at[u])

    def exchange(u):
        columns = pl.ds(pl.multiple_of(other * width + u * STRIP, STRIP), STRIP)
        return pltpu.make_async_remote_copy(
            src_ref=part_ref.at[:, columns], dst_ref=recv.at[u],
            send_sem=xsend_sem.at[u], recv_sem=xrecv_sem.at[u],
            device_id=(me, other), device_id_type=MESH,
        )

    pl.semaphore_signal(barrier, inc=1, device_id=(me, other), device_id_type=MESH)
    each_peer(lambda there: pl.semaphore_signal(barrier, inc=1, device_id=(there, tp), device_id_type=MESH))
    loads = [
        pltpu.make_async_copy(source, place, load_sem.at[i])
        for i, (source, place) in enumerate((
            (dest_in, dest_ref), (pos_in, pos_ref), (slot_in, slot_ref),
            (qscale_in, qscale_ref), (kscale_in, kscale_ref), (freq_in, freq_ref),
        ))
    ]
    loads[0].start()
    nears = [
        pltpu.make_async_copy(
            part_ref.at[:, pl.ds(pl.multiple_of(side_of * width, UNIT), HD)], near.at[:, pl.ds(i * HD, HD)], near_sem.at[i]
        )
        for i, side_of in enumerate((tp, other))
    ]
    for load in nears:
        load.start()
    for u in range(2):
        own_copy(u).start()

    before_ref[...] = (
        lax.broadcasted_iota(jnp.int32, (rows, rows), 0) < lax.broadcasted_iota(jnp.int32, (rows, rows), 1)
    ).astype(f32).astype(bf16)
    loads[0].wait()
    mine = dest_ref[pl.ds(me, 1), :]
    member = mine == lax.broadcasted_iota(jnp.int32, (segments, rows), 0)
    ahead = jnp.dot(member.astype(f32).astype(bf16), before_ref[...], preferred_element_type=f32)
    rank = jnp.sum(jnp.where(member, ahead, 0.0), axis=0, keepdims=True)
    target = mine * CAP + rank.astype(jnp.int32)
    gather_ref[...] = (
        lax.broadcasted_iota(jnp.int32, (rows, rows), 0) == target
    ).astype(f32).astype(bf16)
    acc[...] = jnp.zeros_like(acc)

    for load in nears:
        load.wait()
    moved = jnp.dot(gather_ref[...], near[...], preferred_element_type=f32)
    for i in range(2):
        raw_out[i] = moved[:, i * HD:(i + 1) * HD].reshape(segments, CAP, HD).astype(bf16)
    raw_in[:, pl.ds(me, 1)] = raw_out[:, pl.ds(me, 1)]

    pl.semaphore_wait(barrier, segments)
    exchange(0).start()

    def send_raw(there):
        pltpu.make_async_remote_copy(
            src_ref=raw_out.at[:, there], dst_ref=raw_in.at[:, me], send_sem=raw_send_sem, recv_sem=raw_recv_sem,
            device_id=(there, tp), device_id_type=MESH,
        ).start()

    each_peer(send_raw)
    for u in range(2, strips):
        own_copy(u).start()
    for load in loads[1:]:
        load.start()

    def send(source, target, piece):
        sender = send_sem.at[0 if isinstance(piece, int) and piece < 2 else 1]

        def one(there):
            pltpu.make_async_remote_copy(
                src_ref=source(there), dst_ref=target, send_sem=sender, recv_sem=recv_sem.at[piece],
                device_id=(there, tp), device_id_type=MESH,
            ).start()

        each_peer(one)

    def send_half(i):
        columns = (pl.ds(HD, HD), pl.ds(STRIP, STRIP))[i]
        send(lambda there: outbox.at[0, there, :, columns], inbox.at[0, me, :, columns], i)

    def send_pair(p, carry):
        two = pl.ds(2 * p - 3, 2)
        send(lambda there: outbox.at[two, there], inbox.at[two, me], p)
        return carry

    def reduce_strip(u, carry):
        own_copy(u).wait()
        exchange(u).wait_recv()

        @pl.when(u == 0)
        def _():
            exchange(1).start()
            exchange(2).start()

        @pl.when(u + 3 < strips)
        def _():
            exchange(u + 3).start()

        unit = u // 2
        columns = pl.ds(pl.multiple_of(lax.rem(u, 2) * STRIP, STRIP), STRIP)
        summed = (own[u].astype(f32) + recv[u].astype(f32)).astype(bf16)
        moved = jnp.dot(gather_ref[...], summed, preferred_element_type=f32)
        outbox[unit, :, :, columns] = moved.reshape(segments, CAP, STRIP).astype(bf16)
        square = moved * moved
        acc[...] += square[:, :HD] + square[:, HD:]
        return carry

    lax.fori_loop(0, 1, reduce_strip, 0)
    send_half(0)
    lax.fori_loop(1, 2, reduce_strip, 0)
    send_half(1)
    lax.fori_loop(2, 6, reduce_strip, 0)
    send_pair(2, 0)
    lax.fori_loop(6, 10, reduce_strip, 0)
    send_pair(3, 0)
    every = pl.ds(0, segments - 1)
    pltpu.make_async_copy(raw_in.at[:, every], raw_in.at[:, every], raw_recv_sem).wait()
    swap = pltpu.make_async_remote_copy(
        src_ref=raw_in.at[1], dst_ref=raw_other, send_sem=swap_send_sem, recv_sem=swap_recv_sem,
        device_id=(me, other), device_id_type=MESH,
    )
    swap.start()
    lax.fori_loop(10, strips, reduce_strip, 0)
    mine_too = pl.ds(me, 1)
    inbox[:, mine_too] = outbox[pl.ds(0, units - 1), mine_too]

    lane = lax.broadcasted_iota(jnp.int32, (CAP, HD), 1)
    diagonal = lane == lax.broadcasted_iota(jnp.int32, (CAP, HD), 0)

    def half_rows(i, carry):
        for u in range(8):
            s = i * 8 + u
            tile = acc[pl.ds(pl.multiple_of(s * CAP, CAP), CAP), :]
            column = jnp.sum(tile, axis=1, keepdims=True)
            half[s] = jnp.sum(jnp.where(diagonal, column, 0.0), axis=0, keepdims=True)
        return carry

    lax.fori_loop(0, segments // 8, half_rows, 0)
    halves = pltpu.make_async_remote_copy(
        src_ref=half, dst_ref=half_in, send_sem=hsend_sem, recv_sem=hrecv_sem,
        device_id=(me, other), device_id_type=MESH,
    )
    halves.start()

    arriving = dest_ref[...] == me
    ahead = jnp.dot(arriving.astype(f32).astype(bf16), before_ref[...], preferred_element_type=f32)
    key_ref[...] = jnp.where(arriving, ahead, -1.0)
    halves.wait()
    total[...] = half[...] + half_in[...]

    def send_total(there):
        pltpu.make_async_remote_copy(
            src_ref=total.at[there], dst_ref=total_in.at[me], send_sem=tsend_sem, recv_sem=trecv_sem,
            device_id=(there, tp), device_id_type=MESH,
        ).start()

    each_peer(send_total)
    total_in[pl.ds(me, 1)] = total[pl.ds(me, 1)]

    pairs = units // 2 + 1
    lax.fori_loop(4, pairs, send_pair, 0)

    for load in loads[1:]:
        load.wait()
    scale_ref[0:1, :] = qscale_ref[...] * (math.log2(math.e) / math.sqrt(HD))
    scale_ref[1:2, :] = kscale_ref[...]
    place = lax.broadcasted_iota(jnp.int32, (CAP, rows), 0).astype(f32)
    row_in = lax.broadcasted_iota(jnp.int32, (BLOCK, BLOCK), 0)
    column_in = lax.broadcasted_iota(jnp.int32, (BLOCK, BLOCK), 1)
    same = (row_in // CAP) == (column_in // CAP)
    on_diagonal = row_in == column_in
    half_sign = jnp.where(lax.broadcasted_iota(jnp.int32, (1, HD), 1) < HD // 2, -1.0, 1.0)
    whole = 1.0 / (2 * width)

    def spread(found, row):
        column = jnp.sum(jnp.where(found, row.astype(f32), 0.0), axis=1, keepdims=True)
        return jnp.broadcast_to(column, (CAP, HD))

    def tables(b, carry):
        at = pl.ds(pl.multiple_of(b * BLOCK, BLOCK), BLOCK)
        p = posb[at, :]
        across = jnp.sum(jnp.where(on_diagonal, p, 0.0), axis=0, keepdims=True)
        bias_ref[at, :] = jnp.where(same & (across <= p), 0.0, -1e30)
        angle = p * freq_ref[...]
        cos_ref[at, :] = jnp.cos(angle)
        sin_ref[at, :] = jnp.sin(angle) * half_sign
        return carry

    def inverse_rows(sums):
        def some(i, carry):
            for u in range(8):
                s = i * 8 + u
                column = jnp.sum(jnp.where(diagonal, sums[s], 0.0), axis=1, keepdims=True)
                at = pl.ds(pl.multiple_of(s * CAP, CAP), CAP)
                inv_ref[at, :] = jnp.broadcast_to(lax.rsqrt(column * whole + EPS), (CAP, HD))
            return carry

        lax.fori_loop(0, segments // 8, some, 0)

    leaving = target.astype(f32)
    leaving_pos = pos_ref[pl.ds(me, 1), :]

    def leaving_columns(i, carry):
        for u in range(8):
            s = i * 8 + u
            found = leaving == place + (s * CAP).astype(f32)
            posb[pl.ds(pl.multiple_of(s * CAP, CAP), CAP), :] = spread(found, leaving_pos)
        return carry

    lax.fori_loop(0, segments // 8, leaving_columns, 0)
    lax.fori_loop(0, rows // BLOCK, tables, 0)
    inverse_rows(total)
    last = units - 1

    def store_leaving(at, groups, local, value):
        outbox[last, groups, :, local] = value.reshape(BLOCK // CAP, CAP, HD).astype(bf16)

    attend(
        lambda groups, local: outbox[last, groups, :, local], store_leaving,
        inv_ref, cos_ref, sin_ref, bias_ref, scale_ref, last * UNIT,
    )
    send(lambda there: outbox.at[last, there], last_ref.at[me], pairs)
    last_ref[mine_too] = outbox[last, mine_too]

    def columns_of(i, carry):
        for u in range(8):
            s = i * 8 + u
            found = key_ref[pl.ds(s, 1), :] == place
            at = pl.ds(pl.multiple_of(s * CAP, CAP), CAP)
            posb[at, :] = spread(found, pos_ref[pl.ds(s, 1), :])
            slotb[at, :] = spread(found, slot_ref[pl.ds(s, 1), :])
        return carry

    lax.fori_loop(0, segments // 8, columns_of, 0)
    lax.fori_loop(0, rows // BLOCK, tables, 0)
    slots = lax.broadcasted_iota(jnp.int32, (rows, BLOCK), 0).astype(f32)

    def scatter_block(b, carry):
        at = pl.ds(pl.multiple_of(b * BLOCK, BLOCK), BLOCK)
        goes = jnp.sum(jnp.where(on_diagonal, slotb[at, :], 0.0), axis=0, keepdims=True)
        scatter_ref[:, at] = (slots == goes).astype(f32).astype(bf16)
        return carry

    lax.fori_loop(0, rows // BLOCK, scatter_block, 0)

    every = pl.ds(0, segments - 1)
    pltpu.make_async_copy(total_in.at[every], total_in.at[every], trecv_sem).wait()
    inverse_rows(total_in)

    def arrived(at, piece):
        pltpu.make_async_copy(at, at, recv_sem.at[piece]).wait()

    def attend_unit(unit, carry):
        @pl.when(unit == 0)
        def _():
            arrived(inbox.at[0, every, :, pl.ds(HD, HD)], 0)
            swap.wait_recv()
            inbox[0, :, :, 0:HD] = (raw_in[0].astype(f32) + raw_other[...].astype(f32)).astype(bf16)
            arrived(inbox.at[0, every, :, pl.ds(STRIP, STRIP)], 1)

        @pl.when(lax.rem(unit, 2) == 1)
        def _():
            arrived(inbox.at[pl.ds(unit, 2), every], (unit + 3) // 2)

        def store_arrived(at, groups, local, value):
            att_ref[at, local] = value.astype(bf16)

        first = unit * UNIT
        attend(
            lambda groups, local: inbox[unit, groups, :, local], store_arrived,
            inv_ref, cos_ref, sin_ref, bias_ref, scale_ref, first,
        )
        placed_ref[:, pl.ds(pl.multiple_of(first, UNIT), UNIT)] = jnp.dot(
            scatter_ref[...], att_ref[...], preferred_element_type=f32
        ).astype(bf16)
        return carry

    lax.fori_loop(0, units - 1, attend_unit, 0)
    arrived(last_ref.at[every], pairs)

    for u in range(strips):
        exchange(u).wait_send()
    swap.wait_send()
    pltpu.make_async_copy(raw_out.at[:, every], raw_out.at[:, every], raw_send_sem).wait()
    for i, sent in enumerate((outbox.at[0, every, :, pl.ds(HD, UNIT - HD)], outbox.at[pl.ds(1, units - 1), every])):
        pltpu.make_async_copy(sent, sent, send_sem.at[i]).wait()
    pltpu.make_async_copy(total.at[every], total.at[every], tsend_sem).wait()


def finish(placed_ref, last_ref, scatter_ref, out_ref, tail_ref, copy_sem):
    rows, width = placed_ref.shape
    done = width - UNIT
    early = pltpu.make_async_copy(
        placed_ref.at[:, pl.ds(0, done)], out_ref.at[:, pl.ds(0, done)], copy_sem.at[0]
    )
    early.start()
    arrived = last_ref[...].astype(jnp.float32).reshape(rows, UNIT).astype(jnp.bfloat16)
    tail_ref[...] = jnp.dot(
        scatter_ref[...], arrived, preferred_element_type=jnp.float32
    ).astype(jnp.bfloat16)
    late = pltpu.make_async_copy(tail_ref, out_ref.at[:, pl.ds(done, UNIT)], copy_sem.at[1])
    late.start()
    early.wait()
    late.wait()


def local(partials, kept_positions, destination, slot_index, query_scale, key_scale):
    f32, bf16 = jnp.float32, jnp.bfloat16
    rows, full = partials.shape[2:]
    width = full // 2
    units = width // UNIT
    segments = destination.shape[0]
    side = round(segments ** (1 / 3))
    freq = np.exp(np.arange(HD // 2, dtype=np.float32) * np.float32(-2.0 * math.log(THETA) / HD))
    freq = jnp.asarray(np.concatenate([freq, freq])[None, :].astype(np.float32))
    vmem = pl.BlockSpec(memory_space=pltpu.VMEM)
    hbm = pl.BlockSpec(memory_space=pltpu.HBM)
    sem = pltpu.SemaphoreType.DMA
    strips = 2 * units
    ints = pltpu.VMEM(destination.shape, jnp.int32)
    table = pltpu.VMEM((rows, HD), f32)
    square = pltpu.VMEM((rows, rows), bf16)
    sums = pltpu.VMEM((segments, 1, HD), f32)
    parts = pl.pallas_call(
        functools.partial(kernel, side, rows, width),
        out_shape=[
            pltpu.VMEM((rows, width), bf16),
            pltpu.VMEM((segments, CAP, UNIT), bf16),
            square,
        ],
        in_specs=[hbm] * 7,
        out_specs=[vmem] * 3,
        scratch_shapes=[
            ints, ints, ints,
            pltpu.VMEM((1, width), f32),
            pltpu.VMEM((1, width), f32),
            pltpu.VMEM((1, HD), f32),
            pltpu.VMEM((rows, 2 * HD), bf16),
            pltpu.VMEM((2, segments, CAP, HD), bf16),
            pltpu.VMEM((2, segments, CAP, HD), bf16),
            pltpu.VMEM((segments, CAP, HD), bf16),
            pltpu.VMEM((strips, rows, STRIP), bf16),
            pltpu.VMEM((strips, rows, STRIP), bf16),
            pltpu.VMEM((units, segments, CAP, UNIT), bf16),
            pltpu.VMEM((units - 1, segments, CAP, UNIT), bf16),
            square, square,
            pltpu.VMEM((segments, rows), f32),
            table, table, table, pltpu.VMEM((rows, BLOCK), f32),
            pltpu.VMEM((8, width), f32),
            table, table, table,
            sums, sums, sums, sums,
            pltpu.VMEM((rows, UNIT), bf16),
            sem((strips,)), sem((strips,)), sem((strips,)),
            sem((2,)), sem((units // 2 + 2,)),
            sem, sem, sem, sem,
            sem((6,)),
            sem((2,)), sem, sem, sem, sem,
        ],
        compiler_params=pltpu.CompilerParams(
            collective_id=0, has_side_effects=True, vmem_limit_bytes=36 * 2**20
        ),
        name="handoff",
    )(*(
        pltpu.with_memory_space_constraint(array, pltpu.HBM)
        for array in (
            partials.reshape(rows, full), kept_positions, destination, slot_index,
            query_scale[None, :], key_scale[None, :], freq,
        )
    ))
    return pl.pallas_call(
        finish,
        out_shape=jax.ShapeDtypeStruct((rows, width), bf16),
        in_specs=[vmem] * 3,
        out_specs=pl.BlockSpec(memory_space=pl.ANY),
        scratch_shapes=[
            pltpu.VMEM((rows, UNIT), bf16),
            sem((2,)),
        ],
        compiler_params=pltpu.CompilerParams(vmem_limit_bytes=16 * 2**20),
        name="finish",
    )(*(pltpu.with_memory_space_constraint(part, pltpu.VMEM) for part in parts))


def solution(mesh):
    in_specs = (P("section", "tp", None, None), P(), P(), P(), P("tp"), P("tp"))
    return jax.shard_map(
        local, mesh=mesh, in_specs=in_specs,
        out_specs=P("section", "tp"), check_vma=False,
    )
```

```python
import functools
import math

import jax
import jax.numpy as jnp
import numpy as np
from jax import lax
from jax.experimental import pallas as pl
from jax.experimental.pallas import tpu as pltpu
from jax.sharding import PartitionSpec as P

HD = 128
CAP = 8
EPS = 1e-05
THETA = 500000.0
BLOCK = 128
HEADS = 4
UNIT = HEADS * HD
STRIP = UNIT // 2
MESH = pl.DeviceIdType.MESH


def attend(load, store, inv_ref, cos_ref, sin_ref, bias_ref, scale_ref, first):
    f32, bf16 = jnp.float32, jnp.bfloat16
    rows = inv_ref.shape[0]
    ones = jnp.ones((BLOCK, HD), bf16)
    tiles = []
    for h in range(HEADS):
        local = slice(h * HD, (h + 1) * HD)
        feature = pl.ds(pl.multiple_of(first + h * HD, HD), HD)
        qs = scale_ref[0:1, feature]
        ks = scale_ref[1:2, feature]
        qr = pltpu.roll(qs, HD // 2, 1)
        kr = pltpu.roll(ks, HD // 2, 1)
        for b in range(rows // BLOCK):
            at = slice(b * BLOCK, (b + 1) * BLOCK)
            groups = slice(b * (BLOCK // CAP), (b + 1) * (BLOCK // CAP))
            x = load(groups, local).astype(f32).reshape(BLOCK, HD)
            normed = x * inv_ref[at, :]
            straight = normed * cos_ref[at, :]
            crossed = pltpu.roll(normed, HD // 2, 1) * sin_ref[at, :]
            query = (straight * qs + crossed * qr).astype(bf16)
            keys = (straight * ks + crossed * kr).astype(bf16)
            tiles.append((at, groups, local, query, keys, normed.astype(bf16)))
    scores = [
        lax.dot_general(query, keys, (((1,), (1,)), ((), ())), preferred_element_type=f32)
        for _, _, _, query, keys, _ in tiles
    ]
    weights = []
    for (at, *_), score in zip(tiles, scores):
        score = score + bias_ref[at, :]
        top = jnp.max(score, axis=1, keepdims=True)
        weights.append(jnp.exp2(score - top).astype(bf16))
    sums = [
        jnp.dot(weight, jnp.concatenate([value, ones], axis=1), preferred_element_type=f32)
        for (*_, value), weight in zip(tiles, weights)
    ]
    for (at, groups, local, *_), both in zip(tiles, sums):
        store(at, groups, local, both[:, :HD] / both[:, HD:])


def link_load(offset):
    load = [0] * 6
    for axis, step in enumerate(offset):
        if step in (1, 2):
            load[2 * axis] += 1
        if step in (2, 3):
            load[2 * axis + 1] += 1
    return load


def offset_order(side):
    rest = [(a, b, c) for a in range(side) for b in range(side) for c in range(side)][1:]
    total = [0] * 6
    order = []
    while rest:
        def cost(offset):
            load = link_load(offset)
            after = [t + l for t, l in zip(total, load)]
            mean = sum(after) / 6
            return max(after) - min(after), sum((a - mean) ** 2 for a in after), -sum(load)

        best = min(rest, key=cost)
        rest.remove(best)
        total = [t + l for t, l in zip(total, link_load(best))]
        order.append(best)
    return order


def kernel(
    side, rows, width,
    part_ref, pos_in, dest_in, slot_in, qscale_in, kscale_in, freq_in,
    placed_ref, last_ref, scatter_ref,
    dest_ref, pos_ref, slot_ref, qscale_ref, kscale_ref, freq_ref,
    near, raw_out, raw_in, raw_other,
    own, recv, outbox, inbox, before_ref, gather_ref, key_ref,
    inv_ref, cos_ref, sin_ref, bias_ref, scale_ref,
    posb, slotb, acc, half, half_in, total, total_in, att_ref,
    own_sem, xsend_sem, xrecv_sem, send_sem, recv_sem, hsend_sem, hrecv_sem, tsend_sem, trecv_sem, load_sem,
    near_sem, raw_send_sem, raw_recv_sem, swap_send_sem, swap_recv_sem,
):
    f32, bf16 = jnp.float32, jnp.bfloat16
    segments = side ** 3
    units = width // UNIT
    me = lax.axis_index("section")
    tp = lax.axis_index("tp")
    other = 1 - tp
    strips = width // STRIP
    z, y, x = me // (side * side), lax.rem(me // side, side), lax.rem(me, side)

    order = offset_order(side)

    def each_peer(act):
        for offset in order:
            at = [lax.rem(h + side + o + tp * (side - 2 * o), side) for h, o in zip((z, y, x), offset)]
            act((at[0] * side + at[1]) * side + at[2])

    barrier = pltpu.get_barrier_semaphore()

    def own_copy(u):
        columns = pl.ds(pl.multiple_of(tp * width + u * STRIP, STRIP), STRIP)
        return pltpu.make_async_copy(part_ref.at[:, columns], own.at[u], own_sem.at[u])

    def exchange(u):
        columns = pl.ds(pl.multiple_of(other * width + u * STRIP, STRIP), STRIP)
        return pltpu.make_async_remote_copy(
            src_ref=part_ref.at[:, columns], dst_ref=recv.at[u],
            send_sem=xsend_sem.at[u], recv_sem=xrecv_sem.at[u],
            device_id=(me, other), device_id_type=MESH,
        )

    pl.semaphore_signal(barrier, inc=1, device_id=(me, other), device_id_type=MESH)
    each_peer(lambda there: pl.semaphore_signal(barrier, inc=1, device_id=(there, tp), device_id_type=MESH))
    loads = [
        pltpu.make_async_copy(source, place, load_sem.at[i])
        for i, (source, place) in enumerate((
            (dest_in, dest_ref), (pos_in, pos_ref), (slot_in, slot_ref),
            (qscale_in, qscale_ref), (kscale_in, kscale_ref), (freq_in, freq_ref),
        ))
    ]
    loads[0].start()
    nears = [
        pltpu.make_async_copy(
            part_ref.at[:, pl.ds(pl.multiple_of(side_of * width, UNIT), HD)], near.at[:, pl.ds(i * HD, HD)], near_sem.at[i]
        )
        for i, side_of in enumerate((tp, other))
    ]
    for load in nears:
        load.start()
    for u in range(2):
        own_copy(u).start()

    before_ref[...] = (
        lax.broadcasted_iota(jnp.int32, (rows, rows), 0) < lax.broadcasted_iota(jnp.int32, (rows, rows), 1)
    ).astype(f32).astype(bf16)
    loads[0].wait()
    mine = dest_ref[pl.ds(me, 1), :]
    member = mine == lax.broadcasted_iota(jnp.int32, (segments, rows), 0)
    ahead = jnp.dot(member.astype(f32).astype(bf16), before_ref[...], preferred_element_type=f32)
    rank = jnp.sum(jnp.where(member, ahead, 0.0), axis=0, keepdims=True)
    target = mine * CAP + rank.astype(jnp.int32)
    gather_ref[...] = (
        lax.broadcasted_iota(jnp.int32, (rows, rows), 0) == target
    ).astype(f32).astype(bf16)
    acc[...] = jnp.zeros_like(acc)

    for load in nears:
        load.wait()
    moved = jnp.dot(gather_ref[...], near[...], preferred_element_type=f32)
    for i in range(2):
        raw_out[i] = moved[:, i * HD:(i + 1) * HD].reshape(segments, CAP, HD).astype(bf16)
    raw_in[:, pl.ds(me, 1)] = raw_out[:, pl.ds(me, 1)]

    pl.semaphore_wait(barrier, segments)
    exchange(0).start()

    def send_raw(there):
        pltpu.make_async_remote_copy(
            src_ref=raw_out.at[:, there], dst_ref=raw_in.at[:, me], send_sem=raw_send_sem, recv_sem=raw_recv_sem,
            device_id=(there, tp), device_id_type=MESH,
        ).start()

    each_peer(send_raw)
    for u in range(2, strips):
        own_copy(u).start()
    for load in loads[1:]:
        load.start()

    def send(source, target, piece):
        sender = send_sem.at[0 if isinstance(piece, int) and piece < 2 else 1]

        def one(there):
            pltpu.make_async_remote_copy(
                src_ref=source(there), dst_ref=target, send_sem=sender, recv_sem=recv_sem.at[piece],
                device_id=(there, tp), device_id_type=MESH,
            ).start()

        each_peer(one)

    def send_rest():
        columns = pl.ds(HD, UNIT - HD)
        send(lambda there: outbox.at[0, there, :, columns], inbox.at[0, me, :, columns], 0)

    def send_pair(p, carry):
        two = pl.ds(2 * p - 3, 2)
        send(lambda there: outbox.at[two, there], inbox.at[two, me], p)
        return carry

    def reduce_strip(u, carry):
        own_copy(u).wait()
        exchange(u).wait_recv()

        @pl.when(u == 0)
        def _():
            exchange(1).start()
            exchange(2).start()

        @pl.when(u + 3 < strips)
        def _():
            exchange(u + 3).start()

        unit = u // 2
        columns = pl.ds(pl.multiple_of(lax.rem(u, 2) * STRIP, STRIP), STRIP)
        summed = (own[u].astype(f32) + recv[u].astype(f32)).astype(bf16)
        moved = jnp.dot(gather_ref[...], summed, preferred_element_type=f32)
        outbox[unit, :, :, columns] = moved.reshape(segments, CAP, STRIP).astype(bf16)
        square = moved * moved
        acc[...] += square[:, :HD] + square[:, HD:]
        return carry

    lax.fori_loop(0, 2, reduce_strip, 0)
    send_rest()
    lax.fori_loop(2, 6, reduce_strip, 0)
    send_pair(2, 0)
    lax.fori_loop(6, 10, reduce_strip, 0)
    send_pair(3, 0)
    every = pl.ds(0, segments - 1)
    pltpu.make_async_copy(raw_in.at[:, every], raw_in.at[:, every], raw_recv_sem).wait()
    swap = pltpu.make_async_remote_copy(
        src_ref=raw_in.at[1], dst_ref=raw_other, send_sem=swap_send_sem, recv_sem=swap_recv_sem,
        device_id=(me, other), device_id_type=MESH,
    )
    swap.start()
    lax.fori_loop(10, strips, reduce_strip, 0)
    mine_too = pl.ds(me, 1)
    inbox[:, mine_too] = outbox[pl.ds(0, units - 1), mine_too]

    lane = lax.broadcasted_iota(jnp.int32, (CAP, HD), 1)
    diagonal = lane == lax.broadcasted_iota(jnp.int32, (CAP, HD), 0)

    def half_rows(i, carry):
        for u in range(8):
            s = i * 8 + u
            tile = acc[pl.ds(pl.multiple_of(s * CAP, CAP), CAP), :]
            column = jnp.sum(tile, axis=1, keepdims=True)
            half[s] = jnp.sum(jnp.where(diagonal, column, 0.0), axis=0, keepdims=True)
        return carry

    lax.fori_loop(0, segments // 8, half_rows, 0)
    halves = pltpu.make_async_remote_copy(
        src_ref=half, dst_ref=half_in, send_sem=hsend_sem, recv_sem=hrecv_sem,
        device_id=(me, other), device_id_type=MESH,
    )
    halves.start()

    arriving = dest_ref[...] == me
    ahead = jnp.dot(arriving.astype(f32).astype(bf16), before_ref[...], preferred_element_type=f32)
    key_ref[...] = jnp.where(arriving, ahead, -1.0)
    halves.wait()
    total[...] = half[...] + half_in[...]

    def send_total(there):
        pltpu.make_async_remote_copy(
            src_ref=total.at[there], dst_ref=total_in.at[me], send_sem=tsend_sem, recv_sem=trecv_sem,
            device_id=(there, tp), device_id_type=MESH,
        ).start()

    each_peer(send_total)
    total_in[pl.ds(me, 1)] = total[pl.ds(me, 1)]

    pairs = units // 2 + 1
    lax.fori_loop(4, pairs, send_pair, 0)

    for load in loads[1:]:
        load.wait()
    scale_ref[0:1, :] = qscale_ref[...] * (math.log2(math.e) / math.sqrt(HD))
    scale_ref[1:2, :] = kscale_ref[...]
    place = lax.broadcasted_iota(jnp.int32, (CAP, rows), 0).astype(f32)
    row_in = lax.broadcasted_iota(jnp.int32, (BLOCK, BLOCK), 0)
    column_in = lax.broadcasted_iota(jnp.int32, (BLOCK, BLOCK), 1)
    same = (row_in // CAP) == (column_in // CAP)
    on_diagonal = row_in == column_in
    half_sign = jnp.where(lax.broadcasted_iota(jnp.int32, (1, HD), 1) < HD // 2, -1.0, 1.0)
    whole = 1.0 / (2 * width)

    def spread(found, row):
        column = jnp.sum(jnp.where(found, row.astype(f32), 0.0), axis=1, keepdims=True)
        return jnp.broadcast_to(column, (CAP, HD))

    def tables(b, carry):
        at = pl.ds(pl.multiple_of(b * BLOCK, BLOCK), BLOCK)
        p = posb[at, :]
        across = jnp.sum(jnp.where(on_diagonal, p, 0.0), axis=0, keepdims=True)
        bias_ref[at, :] = jnp.where(same & (across <= p), 0.0, -1e30)
        angle = p * freq_ref[...]
        cos_ref[at, :] = jnp.cos(angle)
        sin_ref[at, :] = jnp.sin(angle) * half_sign
        return carry

    def inverse_rows(sums):
        def some(i, carry):
            for u in range(8):
                s = i * 8 + u
                column = jnp.sum(jnp.where(diagonal, sums[s], 0.0), axis=1, keepdims=True)
                at = pl.ds(pl.multiple_of(s * CAP, CAP), CAP)
                inv_ref[at, :] = jnp.broadcast_to(lax.rsqrt(column * whole + EPS), (CAP, HD))
            return carry

        lax.fori_loop(0, segments // 8, some, 0)

    leaving = target.astype(f32)
    leaving_pos = pos_ref[pl.ds(me, 1), :]

    def leaving_columns(i, carry):
        for u in range(8):
            s = i * 8 + u
            found = leaving == place + (s * CAP).astype(f32)
            posb[pl.ds(pl.multiple_of(s * CAP, CAP), CAP), :] = spread(found, leaving_pos)
        return carry

    lax.fori_loop(0, segments // 8, leaving_columns, 0)
    lax.fori_loop(0, rows // BLOCK, tables, 0)
    inverse_rows(total)
    last = units - 1

    def store_leaving(at, groups, local, value):
        outbox[last, groups, :, local] = value.reshape(BLOCK // CAP, CAP, HD).astype(bf16)

    attend(
        lambda groups, local: outbox[last, groups, :, local], store_leaving,
        inv_ref, cos_ref, sin_ref, bias_ref, scale_ref, last * UNIT,
    )
    send(lambda there: outbox.at[last, there], last_ref.at[me], pairs)
    last_ref[mine_too] = outbox[last, mine_too]

    def columns_of(i, carry):
        for u in range(8):
            s = i * 8 + u
            found = key_ref[pl.ds(s, 1), :] == place
            at = pl.ds(pl.multiple_of(s * CAP, CAP), CAP)
            posb[at, :] = spread(found, pos_ref[pl.ds(s, 1), :])
            slotb[at, :] = spread(found, slot_ref[pl.ds(s, 1), :])
        return carry

    lax.fori_loop(0, segments // 8, columns_of, 0)
    lax.fori_loop(0, rows // BLOCK, tables, 0)
    slots = lax.broadcasted_iota(jnp.int32, (rows, BLOCK), 0).astype(f32)

    def scatter_block(b, carry):
        at = pl.ds(pl.multiple_of(b * BLOCK, BLOCK), BLOCK)
        goes = jnp.sum(jnp.where(on_diagonal, slotb[at, :], 0.0), axis=0, keepdims=True)
        scatter_ref[:, at] = (slots == goes).astype(f32).astype(bf16)
        return carry

    lax.fori_loop(0, rows // BLOCK, scatter_block, 0)

    every = pl.ds(0, segments - 1)
    pltpu.make_async_copy(total_in.at[every], total_in.at[every], trecv_sem).wait()
    inverse_rows(total_in)

    def arrived(at, piece):
        pltpu.make_async_copy(at, at, recv_sem.at[piece]).wait()

    def attend_unit(unit, carry):
        @pl.when(unit == 0)
        def _():
            arrived(inbox.at[0, every, :, pl.ds(HD, UNIT - HD)], 0)
            swap.wait_recv()
            inbox[0, :, :, 0:HD] = (raw_in[0].astype(f32) + raw_other[...].astype(f32)).astype(bf16)

        @pl.when(lax.rem(unit, 2) == 1)
        def _():
            arrived(inbox.at[pl.ds(unit, 2), every], (unit + 3) // 2)

        def store_arrived(at, groups, local, value):
            att_ref[at, local] = value.astype(bf16)

        first = unit * UNIT
        attend(
            lambda groups, local: inbox[unit, groups, :, local], store_arrived,
            inv_ref, cos_ref, sin_ref, bias_ref, scale_ref, first,
        )
        placed_ref[:, pl.ds(pl.multiple_of(first, UNIT), UNIT)] = jnp.dot(
            scatter_ref[...], att_ref[...], preferred_element_type=f32
        ).astype(bf16)
        return carry

    lax.fori_loop(0, units - 1, attend_unit, 0)
    for u in range(strips):
        exchange(u).wait_send()
    swap.wait_send()
    pltpu.make_async_copy(raw_out.at[:, every], raw_out.at[:, every], raw_send_sem).wait()
    pltpu.make_async_copy(total.at[every], total.at[every], tsend_sem).wait()
    arrived(last_ref.at[every], pairs)

    for i, sent in enumerate((outbox.at[0, every, :, pl.ds(HD, UNIT - HD)], outbox.at[pl.ds(1, units - 1), every])):
        pltpu.make_async_copy(sent, sent, send_sem.at[i]).wait()


def finish(placed_ref, last_ref, scatter_ref, out_ref, tail_ref, copy_sem):
    rows, width = placed_ref.shape
    done = width - UNIT
    early = pltpu.make_async_copy(
        placed_ref.at[:, pl.ds(0, done)], out_ref.at[:, pl.ds(0, done)], copy_sem.at[0]
    )
    early.start()
    arrived = last_ref[...].astype(jnp.float32).reshape(rows, UNIT).astype(jnp.bfloat16)
    tail_ref[...] = jnp.dot(
        scatter_ref[...], arrived, preferred_element_type=jnp.float32
    ).astype(jnp.bfloat16)
    late = pltpu.make_async_copy(tail_ref, out_ref.at[:, pl.ds(done, UNIT)], copy_sem.at[1])
    late.start()
    early.wait()
    late.wait()


def local(partials, kept_positions, destination, slot_index, query_scale, key_scale):
    f32, bf16 = jnp.float32, jnp.bfloat16
    rows, full = partials.shape[2:]
    width = full // 2
    units = width // UNIT
    segments = destination.shape[0]
    side = round(segments ** (1 / 3))
    freq = np.exp(np.arange(HD // 2, dtype=np.float32) * np.float32(-2.0 * math.log(THETA) / HD))
    freq = jnp.asarray(np.concatenate([freq, freq])[None, :].astype(np.float32))
    vmem = pl.BlockSpec(memory_space=pltpu.VMEM)
    hbm = pl.BlockSpec(memory_space=pltpu.HBM)
    sem = pltpu.SemaphoreType.DMA
    strips = 2 * units
    ints = pltpu.VMEM(destination.shape, jnp.int32)
    table = pltpu.VMEM((rows, HD), f32)
    square = pltpu.VMEM((rows, rows), bf16)
    sums = pltpu.VMEM((segments, 1, HD), f32)
    parts = pl.pallas_call(
        functools.partial(kernel, side, rows, width),
        out_shape=[
            pltpu.VMEM((rows, width), bf16),
            pltpu.VMEM((segments, CAP, UNIT), bf16),
            square,
        ],
        in_specs=[hbm] * 7,
        out_specs=[vmem] * 3,
        scratch_shapes=[
            ints, ints, ints,
            pltpu.VMEM((1, width), f32),
            pltpu.VMEM((1, width), f32),
            pltpu.VMEM((1, HD), f32),
            pltpu.VMEM((rows, 2 * HD), bf16),
            pltpu.VMEM((2, segments, CAP, HD), bf16),
            pltpu.VMEM((2, segments, CAP, HD), bf16),
            pltpu.VMEM((segments, CAP, HD), bf16),
            pltpu.VMEM((strips, rows, STRIP), bf16),
            pltpu.VMEM((strips, rows, STRIP), bf16),
            pltpu.VMEM((units, segments, CAP, UNIT), bf16),
            pltpu.VMEM((units - 1, segments, CAP, UNIT), bf16),
            square, square,
            pltpu.VMEM((segments, rows), f32),
            table, table, table, pltpu.VMEM((rows, BLOCK), f32),
            pltpu.VMEM((8, width), f32),
            table, table, table,
            sums, sums, sums, sums,
            pltpu.VMEM((rows, UNIT), bf16),
            sem((strips,)), sem((strips,)), sem((strips,)),
            sem((2,)), sem((units // 2 + 2,)),
            sem, sem, sem, sem,
            sem((6,)),
            sem((2,)), sem, sem, sem, sem,
        ],
        compiler_params=pltpu.CompilerParams(
            collective_id=0, has_side_effects=True, vmem_limit_bytes=36 * 2**20
        ),
        name="handoff",
    )(*(
        pltpu.with_memory_space_constraint(array, pltpu.HBM)
        for array in (
            partials.reshape(rows, full), kept_positions, destination, slot_index,
            query_scale[None, :], key_scale[None, :], freq,
        )
    ))
    return pl.pallas_call(
        finish,
        out_shape=jax.ShapeDtypeStruct((rows, width), bf16),
        in_specs=[vmem] * 3,
        out_specs=pl.BlockSpec(memory_space=pl.ANY),
        scratch_shapes=[
            pltpu.VMEM((rows, UNIT), bf16),
            sem((2,)),
        ],
        compiler_params=pltpu.CompilerParams(vmem_limit_bytes=16 * 2**20),
        name="finish",
    )(*(pltpu.with_memory_space_constraint(part, pltpu.VMEM) for part in parts))


def solution(mesh):
    in_specs = (P("section", "tp", None, None), P(), P(), P(), P("tp"), P("tp"))
    return jax.shard_map(
        local, mesh=mesh, in_specs=in_specs,
        out_specs=P("section", "tp"), check_vma=False,
    )
```
